128 devices in a mesh: row: 16 (over x, z), col: 8 (over y, core).
Axes of the slice: x: 4, y: 4, z: 4, core: 2. Of those that a mesh axis runs over, the one named last changes fastest.
Arguments:
- weight: bfloat16 [16384, 39936], P('row', 'col'), may hold values from -8 to 8
- sketch: bfloat16 [39936, 128], P('col'), may hold values from -6 to 6
Outputs:
- factor_a: float32 [16384, 128], P('row')
- factor_b: float32 [128, 39936], P(None, 'col')
- residual: bfloat16 [16384, 39936], P('row', 'col')
The draws below stay inside these ranges and needn't reach their ends.
All inputs are finite; a program needn't handle non-finite values.
Results may differ from the reference program's by a relative error of at most 0.0029.
Values may be sent and summed in bfloat16 or wider, within the bound.
A program may use at most 128 MiB of HBM per device.

```python
import math
import jax
import jax.numpy as jnp
from jax import lax

D = 16384
FF_WIN = 39936
RANK = 128
POWER = 2
NS_ITERS = 12


def draw_weight(key, part):
    key = jax.random.fold_in(key, 11)
    keys = jax.random.split(key, 4)
    left = jax.random.normal(keys[0], (D, RANK), jnp.float32)
    right = jax.random.normal(keys[1], (RANK, FF_WIN), jnp.float32)
    gains = jnp.exp(jax.random.uniform(keys[2], (RANK,), jnp.float32, math.log(3.0), math.log(12.0)))
    noise = jnp.clip(jax.random.normal(keys[3], (D, FF_WIN), jnp.float32), -6.0, 6.0)
    amplitude = gains * ((math.sqrt(D) + math.sqrt(FF_WIN)) / math.sqrt(D * FF_WIN))
    signal = jnp.dot(left * amplitude[None, :], right, precision=lax.Precision.HIGHEST)
    return jnp.clip(signal + noise, -8.0, 8.0).astype(jnp.bfloat16)


def block_levels(key, shape, pieces, low, top_value):
    def one(dim, blocks):
        heights = jax.random.uniform(jax.random.fold_in(jax.random.fold_in(key, 6), dim), (blocks,), jnp.float32, low / len(pieces), top_value / len(pieces))
        return jnp.repeat(jnp.exp(heights), shape[dim] // blocks).reshape((-1,) + (1,) * (len(shape) - dim - 1))

    factor_of = one(*pieces[0])
    for cut in pieces[1:]:
        factor_of = factor_of * one(*cut)
    return factor_of


def scatter_about(own_key, extent, deviation, bound, cuts=(), kind=jnp.bfloat16):
    entries = jax.random.normal(own_key, extent, jnp.float32) * deviation
    if len(cuts) > 0:
        entries = block_levels(own_key, extent, cuts, -0.22, 0.18) * entries
    return jnp.clip(entries, min=-bound, max=bound).astype(kind)


def setup_inputs(seed: int = 0) -> dict:
    key_of = jax.random.split(jax.random.key(seed), 3)
    return {
        "weight": draw_weight(jax.random.fold_in(key_of[2], 71), 0),
        "sketch": scatter_about(key_of[1], (FF_WIN, RANK), 1.0, 6.0, ((0, 8),)),
    }


HIGH = lax.Precision.HIGHEST

def orthonormal(panel):
    for turn in range(2):
        gram = jnp.dot(panel.T.astype(jnp.float32), panel.astype(jnp.float32), precision=HIGH, preferred_element_type=jnp.float32)
        lower = jnp.linalg.cholesky(gram)
        panel = jax.scipy.linalg.solve_triangular(lower, panel.T, lower=True).T
    return panel

def sqrt_pair(matrix):
    scale = jnp.sqrt(jnp.sum(matrix * matrix))
    eye = jnp.eye(matrix.shape[0], dtype=jnp.float32)
    upper = matrix / scale
    inverse = eye
    for turn in range(NS_ITERS):
        middle = 1.5 * eye - 0.5 * jnp.dot(inverse, upper, precision=HIGH)
        upper = jnp.dot(upper, middle, precision=HIGH)
        inverse = jnp.dot(middle, inverse, precision=HIGH)
    return (upper * jnp.sqrt(scale), inverse / jnp.sqrt(scale))

def reference(weight, sketch):
    factor = sketch
    for step in range(POWER + 1):
        tall = jnp.dot(weight.astype(jnp.float32), factor.astype(jnp.float32), preferred_element_type=jnp.float32)
        basis = orthonormal(tall)
        wide = lax.dot_general(weight.astype(jnp.float32), basis.astype(jnp.bfloat16).astype(jnp.float32), (((0,), (0,)), ((), ())), preferred_element_type=jnp.float32)
        if step < POWER:
            factor = orthonormal(wide).astype(jnp.bfloat16)
    gram = jnp.dot(wide.T.astype(jnp.float32), wide.astype(jnp.float32), precision=HIGH, preferred_element_type=jnp.float32)
    half, inv_half = sqrt_pair(gram)
    quarter, inv_quarter = sqrt_pair(half)
    factor_a = jnp.dot(basis, quarter, precision=HIGH)
    factor_b = jnp.dot(inv_quarter, wide.T, precision=HIGH)
    block = math.gcd(D, 512)
    blocks_w = weight.reshape(D // block, block, FF_WIN)
    blocks_a = factor_a.reshape(D // block, block, RANK)

    def one_block(pair):
        return (pair[0].astype(jnp.float32) - jnp.dot(pair[1], factor_b, precision=HIGH)).astype(jnp.bfloat16)
    residual = lax.map(one_block, (blocks_w, blocks_a)).reshape(D, FF_WIN)
    return (factor_a, factor_b, residual)
```

```python
import jax
import jax.numpy as jnp
from jax import lax
from jax.experimental import pallas as pl
from jax.experimental.pallas import tpu as pltpu
from jax.sharding import PartitionSpec as P

POWER = 2
NS_ITERS = 12
RANK = 128
ROWS = 1024
COLS = 4992
PAD = 5120
NCOL = 8
NROW = 16
PART = PAD // 4
OWN = PAD // NROW
PIECE = PART // NROW
TALL = ROWS // NCOL
SEG = RANK // NCOL
STEPS = POWER + 1
TILE = 384

f32 = jnp.float32
bf16 = jnp.bfloat16
MESH = pl.DeviceIdType.MESH

ORDER = ((0, 2, 1, 3), (2, 1, 3, 0), (1, 3, 0, 2), (3, 0, 2, 1))


def split3(a):
    hi = a.astype(bf16)
    rest = a - hi.astype(f32)
    mid = rest.astype(bf16)
    low = (rest - mid.astype(f32)).astype(bf16)
    return hi, mid, low


def left6(a, axis):
    hi, mid, low = split3(a)
    return jnp.concatenate([hi, hi, mid, hi, low, mid], axis)


def right6(a, axis):
    hi, mid, low = split3(a)
    return jnp.concatenate([hi, mid, hi, low, hi, mid], axis)


def mm(a, b):
    return jnp.dot(left6(a, 1), right6(b, 0), preferred_element_type=f32)


def gram_of(y):
    return lax.dot_general(
        left6(y, 0), right6(y, 0), (((0,), (0,)), ((), ())), preferred_element_type=f32
    )


def eye_of():
    r = lax.broadcasted_iota(jnp.int32, (RANK, RANK), 0)
    c = lax.broadcasted_iota(jnp.int32, (RANK, RANK), 1)
    return jnp.where(r == c, 1.0, 0.0).astype(f32)


def cholesky_inverse(gram, s_ref, m_ref, hook):
    s_ref[:, 0:RANK] = gram
    s_ref[:, RANK:] = eye_of()
    sub = lax.broadcasted_iota(jnp.int32, (8, RANK), 0)
    lane = lax.broadcasted_iota(jnp.int32, (8, RANK), 1)
    for k in range(RANK // 8):
        o = 8 * k
        hook(k)
        a_rows = s_ref[o : o + 8, 0:RANK]
        n_rows = s_ref[o : o + 8, RANK:]
        d = [[None] * 8 for _ in range(8)]
        l = [[None] * 8 for _ in range(8)]
        inv = [None] * 8
        for j in range(8):
            column = jnp.broadcast_to(a_rows[:, o + j : o + j + 1], (8, RANK))
            for i in range(j, 8):
                d[i][j] = jnp.broadcast_to(column[i : i + 1, :], (8, RANK))
        for j in range(8):
            inv[j] = lax.rsqrt(d[j][j])
            for i in range(j + 1, 8):
                l[i][j] = d[i][j] * inv[j]
            for i in range(j + 1, 8):
                for c in range(j + 1, i + 1):
                    d[i][c] = d[i][c] - l[i][j] * l[c][j]
        ua = [None] * 8
        un = [None] * 8
        u = jnp.zeros((8, RANK), f32)
        n = jnp.zeros((8, RANK), f32)
        for i in range(8):
            a = jnp.broadcast_to(a_rows[i : i + 1, :], (8, RANK))
            b = jnp.broadcast_to(n_rows[i : i + 1, :], (8, RANK))
            for c in range(i):
                a = a - l[i][c] * ua[c]
                b = b - l[i][c] * un[c]
            ua[i] = a * inv[i]
            un[i] = b * inv[i]
            u = jnp.where(sub == i, ua[i], u)
            n = jnp.where(sub == i, un[i], n)
        m_ref[o : o + 8, :] = n
        if o + 8 < RANK:
            u = jnp.where(lane >= o + 8, u, 0.0)
            parts = []
            for v in (u, n):
                hi = v.astype(bf16).astype(f32)
                mid = (v - hi).astype(bf16).astype(f32)
                parts.append((hi, mid, v - hi - mid))
            (uh, um, ul), (nh, nm, nl) = parts
            left = jnp.concatenate([uh, uh, um, uh, ul, um], 0)
            right = jnp.concatenate(
                [
                    jnp.concatenate([uh, um, uh, ul, uh, um], 0),
                    jnp.concatenate([nh, nm, nh, nl, nh, nm], 0),
                ],
                1,
            )
            change = lax.dot_general(
                left, right, (((0,), (0,)), ((), ())), preferred_element_type=f32
            )
            s_ref[o + 8 :, :] = s_ref[o + 8 :, :] - change[o + 8 :, :]


def factors_kernel(
    w_hbm, sketch_ref, basis_ref, wide_ref, q_ref, iq_ref,
    w_ref, fac, b16, part, tall_in, tall_all, rb0, rb1, rb2, rb3, wide_all,
    own, g_ref, ar1, ar2, ar3, s_ref, m_ref, total_ref, y_ref,
    w_sem, ar_send, ar_recv, t_send, t_recv, ta_send, ta_recv, r_send, r_recv, a_send, a_recv,
):
    row = lax.axis_index("row")
    col = lax.axis_index("col")
    y = col // 2
    x = row // 4
    z = row % 4
    partner = ((x + 1 - 2 * (x % 2)) * 4 + z, (3 - x) * 4 + z, x * 4 + z + 1 - 2 * (z % 2), x * 4 + 3 - z)
    xhi, zhi = x // 2, z // 2
    bit = ((x + xhi) % 2, xhi, (z + zhi) % 2, zhi)

    w_copy = pltpu.make_async_copy(w_hbm, w_ref.at[:, pl.ds(0, COLS)], w_sem)
    w_copy.start()

    barrier = pltpu.get_barrier_semaphore()
    for d in range(1, NCOL):
        pl.semaphore_signal(barrier, inc=1, device_id={"col": (col + d) % NCOL}, device_id_type=MESH)
    for d in range(1, NROW):
        pl.semaphore_signal(barrier, inc=1, device_id={"row": (row + d) % NROW}, device_id_type=MESH)

    w_ref[:, pl.ds(COLS, PAD - COLS)] = jnp.zeros((ROWS, PAD - COLS), bf16)
    fac[pl.ds(0, COLS), :] = sketch_ref[...]
    fac[pl.ds(COLS, PAD - COLS), :] = jnp.zeros((PAD - COLS, RANK), bf16)
    pl.semaphore_wait(barrier, NCOL + NROW - 2)
    w_copy.wait()

    def send(src, dst, send_sem, recv_sem, to):
        pltpu.make_async_remote_copy(
            src_ref=src, dst_ref=dst, send_sem=send_sem, recv_sem=recv_sem, device_id=to, device_id_type=MESH
        ).start()

    def wait(ref, sem):
        pltpu.make_async_copy(ref, ref, sem).wait()

    def all_reduce(index):
        first, second, third = ar1.at[index], ar2.at[index], ar3.at[index]
        for d in range(1, NCOL):
            peer = (col + d) % NCOL
            send(g_ref.at[pl.ds(pl.multiple_of(peer * SEG, SEG), SEG), :], first.at[col],
                 ar_send.at[index, 0], ar_recv.at[index, 0], {"col": peer})
        mine = pl.ds(pl.multiple_of(col * SEG, SEG), SEG)
        first[col] = g_ref[mine, :]
        wait(first.at[pl.ds(0, NCOL - 1)], ar_recv.at[index, 0])
        second[row] = jnp.sum(first[...], axis=0)
        for d in range(1, NROW):
            send(second.at[row], second.at[row], ar_send.at[index, 1], ar_recv.at[index, 1],
                 {"row": (row + d) % NROW})
        wait(second.at[pl.ds(0, NROW - 1)], ar_recv.at[index, 1])
        third[mine, :] = jnp.sum(second[...], axis=0)
        for d in range(1, NCOL):
            send(third.at[mine, :], third.at[mine, :], ar_send.at[index, 2], ar_recv.at[index, 2],
                 {"col": (col + d) % NCOL})
        wait(third.at[pl.ds(0, SEG * (NCOL - 1)), :], ar_recv.at[index, 2])
        wait(first.at[pl.ds(0, NCOL - 1)], ar_send.at[index, 0])
        wait(second.at[pl.ds(0, NROW - 1)], ar_send.at[index, 1])
        wait(third.at[pl.ds(0, SEG * (NCOL - 1)), :], ar_send.at[index, 2])

    def orth(rows, base, hook):
        def one(turn, carry):
            panel = own[pl.ds(0, rows), :]
            g_ref[...] = gram_of(panel)
            all_reduce(base + turn)
            cholesky_inverse(ar3[base + turn], s_ref, m_ref, lambda k: hook(turn, k))
            inverse = m_ref[...]

            @pl.when(turn == 0)
            def _():
                total_ref[...] = inverse.T
                own[pl.ds(0, rows), :] = mm(own[pl.ds(0, rows), :], inverse.T)

            @pl.when(turn == 1)
            def _():
                total_ref[...] = mm(total_ref[...], inverse.T)

            return carry

        lax.fori_loop(0, 2, one, 0)

    def step(k, carry):
        mine = pl.ds(pl.multiple_of(col * TALL, TALL), TALL)
        tall_k = tall_in.at[k]

        def tall_pair(j, carry):
            pair = (y + 1 + j) % 4
            at = pl.ds(pl.multiple_of(pair * 2 * TALL, 2 * TALL), 2 * TALL)
            y_ref[at, :] = jnp.dot(w_ref[at, :], fac[...], preferred_element_type=f32)

            @pl.when(j < 3)
            def _():
                for core in range(2):
                    peer = pair * 2 + core
                    send(y_ref.at[pl.ds(pl.multiple_of(peer * TALL, TALL), TALL), :], tall_k.at[col],
                         t_send.at[k], t_recv.at[k], {"col": peer})

            return carry

        lax.fori_loop(0, 4, tall_pair, 0)
        peer = col + 1 - 2 * (col % 2)
        send(y_ref.at[pl.ds(pl.multiple_of(peer * TALL, TALL), TALL), :], tall_k.at[col],
             t_send.at[k], t_recv.at[k], {"col": peer})
        tall_k[col] = y_ref[mine, :]
        wait(tall_k.at[pl.ds(0, NCOL - 1)], t_recv.at[k])
        wait(tall_k.at[pl.ds(0, NCOL - 1)], t_send.at[k])
        panel = jnp.sum(tall_k[...], axis=0)
        own[pl.ds(0, TALL), :] = panel
        whole = tall_all.at[k]
        whole[mine, :] = panel

        def tall_hook(turn, block):
            if block == 0:

                @pl.when(turn == 0)
                def _():
                    for d in range(1, NCOL):
                        send(whole.at[mine, :], whole.at[mine, :], ta_send.at[k], ta_recv.at[k],
                             {"col": (col + d) % NCOL})

        orth(TALL, k * 4, tall_hook)
        wait(whole.at[pl.ds(0, TALL * (NCOL - 1)), :], ta_recv.at[k])
        wait(whole.at[pl.ds(0, TALL * (NCOL - 1)), :], ta_send.at[k])

        def make_basis(t, carry):
            at = pl.ds(pl.multiple_of(t * 256, 256), 256)
            basis = mm(whole[at, :], total_ref[...])
            basis_ref[at, :] = basis
            b16[at, :] = basis.astype(bf16)
            return carry

        lax.fori_loop(0, ROWS // 256, make_basis, 0)

        buffers = (rb0.at[k], rb1.at[k], rb2.at[k], rb3.at[k])
        start = [PART * q for q in range(4)]

        def times(at):
            part[at, :] = lax.dot_general(
                w_ref[:, at], b16[...], (((0,), (0,)), ((), ())), preferred_element_type=f32
            )

        def rows_at(offset, size):
            return pl.ds(pl.multiple_of(offset, PIECE), size)

        size = PART
        for s in range(4):
            size = size // 2
            for q in range(4):
                kind = ORDER[q][s]
                at = rows_at(start[q] + (1 - bit[kind]) * size, size)
                if s == 0:
                    at = pl.ds(pl.multiple_of(start[q] + (1 - bit[kind]) * size, 128), size)
                    times(at)
                send(part.at[at, :], buffers[s].at[q], r_send.at[k, s, q], r_recv.at[k, s, q],
                     {"row": partner[kind]})
            for q in range(4):
                kind = ORDER[q][s]
                start[q] = start[q] + bit[kind] * size
                if s == 0:
                    times(pl.ds(pl.multiple_of(start[q], 128), size))
            for q in range(4):
                at = rows_at(start[q], size)
                wait(buffers[s].at[q], r_recv.at[k, s, q])
                part[at, :] = part[at, :] + buffers[s][q]
        for s in range(4):
            for q in range(4):
                wait(buffers[s].at[q], r_send.at[k, s, q])
        wide_k = wide_all.at[k]
        for q in range(4):
            at = rows_at(start[q], PIECE)
            own[pl.ds(PIECE * q, PIECE), :] = part[at, :]
            wide_k[at, :] = part[at, :]

        place = [list(start)]
        for j in range(4):
            now = list(place[-1])
            for q in range(4):
                now[q] = now[q] - bit[ORDER[q][3 - j]] * (PIECE << j)
            place.append(now)

        def gather_start(j):
            for q in range(4):
                at = rows_at(place[j][q], PIECE << j)
                send(wide_k.at[at, :], wide_k.at[at, :], a_send.at[k, j, q], a_recv.at[k, j, q],
                     {"row": partner[ORDER[q][3 - j]]})

        def gather_wait(j):
            for q in range(4):
                ref = wide_k.at[pl.ds(0, PIECE << j), :]
                wait(ref, a_recv.at[k, j, q])
                wait(ref, a_send.at[k, j, q])

        @pl.when(k < POWER)
        def _():
            def wide_hook(turn, block):
                if block in (0, 5, 10):

                    @pl.when(turn == 0)
                    def _():
                        if block:
                            gather_wait(block // 5 - 1)
                        gather_start(block // 5)

                if block == 0:

                    @pl.when(turn == 1)
                    def _():
                        gather_wait(2)
                        gather_start(3)

            orth(OWN, k * 4 + 2, wide_hook)
            gather_wait(3)

            def make_factor(t, carry):
                at = pl.ds(pl.multiple_of(t * 512, 512), 512)
                fac[at, :] = mm(wide_k[at, :], total_ref[...]).astype(bf16)
                return carry

            lax.fori_loop(0, PAD // 512, make_factor, 0)

        @pl.when(k == POWER)
        def _():
            g_ref[...] = gram_of(own[...])
            all_reduce(k * 4 + 2)
            gather_start(0)
            eye = eye_of()

            def newton(_, pair):
                upper, inverse = pair
                middle = 1.5 * eye - 0.5 * mm(inverse, upper)
                return mm(upper, middle), mm(middle, inverse)

            def sqrt_pair(matrix, hook):
                scale = jnp.sqrt(jnp.sum(matrix * matrix, keepdims=True))
                pair = (matrix / scale, eye)
                for third in range(3):
                    pair = lax.fori_loop(0, NS_ITERS // 3, newton, pair)
                    hook(third)
                root = jnp.sqrt(scale)
                return pair[0] * root, pair[1] / root

            def first(third):
                gather_wait(third)
                gather_start(third + 1)

            half, _ = sqrt_pair(ar3[k * 4 + 2], first)
            quarter, inv_quarter = sqrt_pair(half, lambda third: None)
            q_ref[...] = quarter
            iq_ref[...] = inv_quarter
            gather_wait(3)
            wide_ref[...] = wide_k[...]

        return carry

    lax.fori_loop(0, STEPS, step, 0)


def factors(weight, sketch):
    vmem = pl.BlockSpec(memory_space=pltpu.VMEM)
    dma = pltpu.SemaphoreType.DMA
    return pl.pallas_call(
        factors_kernel,
        name="factors",
        out_shape=(
            jax.ShapeDtypeStruct((ROWS, RANK), f32),
            jax.ShapeDtypeStruct((PAD, RANK), f32),
            jax.ShapeDtypeStruct((RANK, RANK), f32),
            jax.ShapeDtypeStruct((RANK, RANK), f32),
        ),
        in_specs=[pl.BlockSpec(memory_space=pl.ANY), vmem],
        out_specs=(vmem, vmem, vmem, vmem),
        scratch_shapes=[
            pltpu.VMEM((ROWS, PAD), bf16),
            pltpu.VMEM((PAD, RANK), bf16),
            pltpu.VMEM((ROWS, RANK), bf16),
            pltpu.VMEM((PAD, RANK), f32),
            pltpu.VMEM((STEPS, NCOL, TALL, RANK), f32),
            pltpu.VMEM((STEPS, ROWS, RANK), f32),
            pltpu.VMEM((STEPS, 4, PART // 2, RANK), f32),
            pltpu.VMEM((STEPS, 4, PART // 4, RANK), f32),
            pltpu.VMEM((STEPS, 4, PART // 8, RANK), f32),
            pltpu.VMEM((STEPS, 4, PART // 16, RANK), f32),
            pltpu.VMEM((STEPS, PAD, RANK), f32),
            pltpu.VMEM((OWN, RANK), f32),
            pltpu.VMEM((RANK, RANK), f32),
            pltpu.VMEM((STEPS * 4, NCOL, SEG, RANK), f32),
            pltpu.VMEM((STEPS * 4, NROW, SEG, RANK), f32),
            pltpu.VMEM((STEPS * 4, RANK, RANK), f32),
            pltpu.VMEM((RANK, 2 * RANK), f32),
            pltpu.VMEM((RANK, RANK), f32),
            pltpu.VMEM((RANK, RANK), f32),
            pltpu.VMEM((ROWS, RANK), f32),
            dma,
            dma((STEPS * 4, 3)),
            dma((STEPS * 4, 3)),
            dma((STEPS,)),
            dma((STEPS,)),
            dma((STEPS,)),
            dma((STEPS,)),
            dma((STEPS, 4, 4)),
            dma((STEPS, 4, 4)),
            dma((STEPS, 4, 4)),
            dma((STEPS, 4, 4)),
        ],
        compiler_params=pltpu.CompilerParams(
            collective_id=0, has_side_effects=True, vmem_limit_bytes=60 << 20
        ),
    )(weight, sketch)


def residual_kernel(w_ref, basis_ref, q_ref, iq_ref, wide_ref, fa_ref, fb_ref, res_ref, left):
    @pl.when(pl.program_id(0) == 0)
    def _():
        for t in range(ROWS // 256):
            at = pl.ds(t * 256, 256)
            a = mm(basis_ref[at, :], q_ref[...])
            fa_ref[at, :] = a
            hi = a.astype(bf16)
            low = (a - hi.astype(f32)).astype(bf16)
            left[at, :] = jnp.concatenate([hi, low, hi, low], 1)

    b = mm(iq_ref[...], wide_ref[...].T)
    fb_ref[...] = b
    hi = b.astype(bf16)
    low = (b - hi.astype(f32)).astype(bf16)
    product = jnp.dot(left[...], jnp.concatenate([hi, hi, low, low], 0), preferred_element_type=f32)
    res_ref[...] = (w_ref[...].astype(f32) - product).astype(bf16)


def residual(weight, basis, quarter, inv_quarter, wide):
    small = pl.BlockSpec((RANK, RANK), lambda i: (0, 0))
    panel = pl.BlockSpec((ROWS, RANK), lambda i: (0, 0))
    block = pl.BlockSpec((ROWS, TILE), lambda i: (0, i))
    return pl.pallas_call(
        residual_kernel,
        name="residual",
        grid=(COLS // TILE,),
        out_shape=(
            jax.ShapeDtypeStruct((ROWS, RANK), f32),
            jax.ShapeDtypeStruct((RANK, COLS), f32),
            jax.ShapeDtypeStruct((ROWS, COLS), bf16),
        ),
        in_specs=[block, panel, small, small, pl.BlockSpec((TILE, RANK), lambda i: (i, 0))],
        out_specs=(panel, pl.BlockSpec((RANK, TILE), lambda i: (0, i)), block),
        scratch_shapes=[pltpu.VMEM((ROWS, 4 * RANK), bf16)],
        compiler_params=pltpu.CompilerParams(vmem_limit_bytes=60 << 20),
    )(weight, basis, quarter, inv_quarter, wide)


def on_device(weight, sketch):
    basis, wide, quarter, inv_quarter = factors(weight, sketch)
    return residual(weight, basis, quarter, inv_quarter, wide)


def solution(mesh):
    return jax.shard_map(
        on_device,
        mesh=mesh,
        in_specs=(P("row", "col"), P("col", None)),
        out_specs=(P("row", None), P(None, "col"), P("row", "col")),
        check_vma=False,
    )
```

```python
import jax
import jax.numpy as jnp
from jax import lax
from jax.experimental import pallas as pl
from jax.experimental.pallas import tpu as pltpu
from jax.sharding import PartitionSpec as P

POWER = 2
NS_ITERS = 12
RANK = 128
ROWS = 1024
COLS = 4992
PAD = 5120
NCOL = 8
NROW = 16
PART = PAD // 4
OWN = PAD // NROW
PIECE = PART // NROW
TALL = ROWS // NCOL
SEG = RANK // NCOL
STEPS = POWER + 1
TILE = 384

f32 = jnp.float32
bf16 = jnp.bfloat16
MESH = pl.DeviceIdType.MESH

ORDER = ((0, 2, 1, 3), (2, 1, 3, 0), (1, 3, 0, 2), (3, 0, 2, 1))


def split3(a):
    hi = a.astype(bf16)
    rest = a - hi.astype(f32)
    mid = rest.astype(bf16)
    low = (rest - mid.astype(f32)).astype(bf16)
    return hi, mid, low


def left6(a, axis):
    hi, mid, low = split3(a)
    return jnp.concatenate([hi, hi, mid, hi, low, mid], axis)


def right6(a, axis):
    hi, mid, low = split3(a)
    return jnp.concatenate([hi, mid, hi, low, hi, mid], axis)


def mm(a, b):
    return jnp.dot(left6(a, 1), right6(b, 0), preferred_element_type=f32)


def gram_of(y):
    return lax.dot_general(
        left6(y, 0), right6(y, 0), (((0,), (0,)), ((), ())), preferred_element_type=f32
    )


def eye_of():
    r = lax.broadcasted_iota(jnp.int32, (RANK, RANK), 0)
    c = lax.broadcasted_iota(jnp.int32, (RANK, RANK), 1)
    return jnp.where(r == c, 1.0, 0.0).astype(f32)


def cholesky_inverse(gram, s_ref, m_ref):
    s_ref[:, 0:RANK] = gram
    s_ref[:, RANK:] = eye_of()
    sub = lax.broadcasted_iota(jnp.int32, (8, RANK), 0)
    lane = lax.broadcasted_iota(jnp.int32, (8, RANK), 1)
    for k in range(RANK // 8):
        o = 8 * k
        a_rows = s_ref[o : o + 8, 0:RANK]
        n_rows = s_ref[o : o + 8, RANK:]
        d = [[None] * 8 for _ in range(8)]
        l = [[None] * 8 for _ in range(8)]
        inv = [None] * 8
        for j in range(8):
            column = jnp.broadcast_to(a_rows[:, o + j : o + j + 1], (8, RANK))
            for i in range(j, 8):
                d[i][j] = jnp.broadcast_to(column[i : i + 1, :], (8, RANK))
        for j in range(8):
            inv[j] = lax.rsqrt(d[j][j])
            for i in range(j + 1, 8):
                l[i][j] = d[i][j] * inv[j]
            for i in range(j + 1, 8):
                for c in range(j + 1, i + 1):
                    d[i][c] = d[i][c] - l[i][j] * l[c][j]
        ua = [None] * 8
        un = [None] * 8
        u = jnp.zeros((8, RANK), f32)
        n = jnp.zeros((8, RANK), f32)
        for i in range(8):
            a = jnp.broadcast_to(a_rows[i : i + 1, :], (8, RANK))
            b = jnp.broadcast_to(n_rows[i : i + 1, :], (8, RANK))
            for c in range(i):
                a = a - l[i][c] * ua[c]
                b = b - l[i][c] * un[c]
            ua[i] = a * inv[i]
            un[i] = b * inv[i]
            u = jnp.where(sub == i, ua[i], u)
            n = jnp.where(sub == i, un[i], n)
        m_ref[o : o + 8, :] = n
        if o + 8 < RANK:
            u = jnp.where(lane >= o + 8, u, 0.0)
            parts = []
            for v in (u, n):
                hi = v.astype(bf16).astype(f32)
                mid = (v - hi).astype(bf16).astype(f32)
                parts.append((hi, mid, v - hi - mid))
            (uh, um, ul), (nh, nm, nl) = parts
            left = jnp.concatenate([uh, uh, um, uh, ul, um], 0)
            right = jnp.concatenate(
                [
                    jnp.concatenate([uh, um, uh, ul, uh, um], 0),
                    jnp.concatenate([nh, nm, nh, nl, nh, nm], 0),
                ],
                1,
            )
            change = lax.dot_general(
                left, right, (((0,), (0,)), ((), ())), preferred_element_type=f32
            )
            s_ref[o + 8 :, :] = s_ref[o + 8 :, :] - change[o + 8 :, :]


def factors_kernel(
    w_hbm, sketch_ref, basis_ref, wide_ref, q_ref, iq_ref,
    w_ref, fac, b16, part, tall_in, tall_all, rb0, rb1, rb2, rb3, wide_all,
    own, g_ref, ar1, ar2, ar3, s_ref, m_ref, total_ref, second_ref, y_ref,
    w_sem, ar_send, ar_recv, t_send, t_recv, ta_send, ta_recv, r_send, r_recv, a_send, a_recv,
):
    row = lax.axis_index("row")
    col = lax.axis_index("col")
    y = col // 2
    x = row // 4
    z = row % 4
    partner = ((x + 1 - 2 * (x % 2)) * 4 + z, (3 - x) * 4 + z, x * 4 + z + 1 - 2 * (z % 2), x * 4 + 3 - z)
    xhi, zhi = x // 2, z // 2
    bit = ((x + xhi) % 2, xhi, (z + zhi) % 2, zhi)

    def load(j):
        at = pl.ds(pl.multiple_of((y + 1 + j) % 4 * 2 * TALL, 2 * TALL), 2 * TALL)
        return pltpu.make_async_copy(w_hbm.at[at, :], w_ref.at[at, pl.ds(0, COLS)], w_sem.at[j])

    for j in range(4):
        load(j).start()

    barrier = pltpu.get_barrier_semaphore()
    for d in range(1, NCOL):
        pl.semaphore_signal(barrier, inc=1, device_id={"col": (col + d) % NCOL}, device_id_type=MESH)
    for d in range(1, NROW):
        pl.semaphore_signal(barrier, inc=1, device_id={"row": (row + d) % NROW}, device_id_type=MESH)

    w_ref[:, pl.ds(COLS, PAD - COLS)] = jnp.zeros((ROWS, PAD - COLS), bf16)
    fac[pl.ds(0, COLS), :] = sketch_ref[...]
    fac[pl.ds(COLS, PAD - COLS), :] = jnp.zeros((PAD - COLS, RANK), bf16)
    pl.semaphore_wait(barrier, NCOL + NROW - 2)

    def send(src, dst, send_sem, recv_sem, to):
        pltpu.make_async_remote_copy(
            src_ref=src, dst_ref=dst, send_sem=send_sem, recv_sem=recv_sem, device_id=to, device_id_type=MESH
        ).start()

    def wait(ref, sem):
        pltpu.make_async_copy(ref, ref, sem).wait()

    mine16 = pl.ds(pl.multiple_of(col * SEG, SEG), SEG)

    def sum_start(index):
        for d in range(1, NCOL):
            peer = (col + d) % NCOL
            send(g_ref.at[index, pl.ds(pl.multiple_of(peer * SEG, SEG), SEG), :], ar1.at[index, col],
                 ar_send.at[index, 0], ar_recv.at[index, 0], {"col": peer})
        ar1[index, col] = g_ref[index, mine16, :]

    def sum_row(index):
        wait(ar1.at[index, pl.ds(0, NCOL - 1)], ar_recv.at[index, 0])
        ar2[index, row] = jnp.sum(ar1[index], axis=0)
        for d in range(1, NROW):
            send(ar2.at[index, row], ar2.at[index, row], ar_send.at[index, 1], ar_recv.at[index, 1],
                 {"row": (row + d) % NROW})

    def sum_col(index):
        wait(ar2.at[index, pl.ds(0, NROW - 1)], ar_recv.at[index, 1])
        ar3[index, mine16, :] = jnp.sum(ar2[index], axis=0)
        for d in range(1, NCOL):
            send(ar3.at[index, mine16, :], ar3.at[index, mine16, :], ar_send.at[index, 2], ar_recv.at[index, 2],
                 {"col": (col + d) % NCOL})

    def sum_end(index):
        wait(ar3.at[index, pl.ds(0, SEG * (NCOL - 1)), :], ar_recv.at[index, 2])
        wait(ar1.at[index, pl.ds(0, NCOL - 1)], ar_send.at[index, 0])
        wait(ar2.at[index, pl.ds(0, NROW - 1)], ar_send.at[index, 1])
        wait(ar3.at[index, pl.ds(0, SEG * (NCOL - 1)), :], ar_send.at[index, 2])

    def first_pass(index, rows, second_index):
        second = second_ref[...]
        gram = mm(mm(second, ar3[index]), second.T)
        cholesky_inverse(gram, s_ref, m_ref)
        total = mm(m_ref[...], second).T
        total_ref[...] = total
        g_ref[second_index] = gram_of(mm(own[pl.ds(0, rows), :], total))
        sum_start(second_index)

    def second_pass(index):
        sum_end(index)
        cholesky_inverse(ar3[index], s_ref, second_ref)

    second_ref[...] = eye_of()

    def step(k, carry):
        first_tall, second_tall, first_wide, second_wide = (k * 4 + i for i in range(4))
        last_wide = jnp.maximum(k - 1, 0) * 4 + 3

        mine = pl.ds(pl.multiple_of(col * TALL, TALL), TALL)
        tall_k = tall_in.at[k]

        def tall_pair(j, carry):
            pair = (y + 1 + j) % 4
            at = pl.ds(pl.multiple_of(pair * 2 * TALL, 2 * TALL), 2 * TALL)

            @pl.when(k == 0)
            def _():
                load(j).wait()

            y_ref[at, :] = jnp.dot(w_ref[at, :], fac[...], preferred_element_type=f32)

            @pl.when(j < 3)
            def _():
                for core in range(2):
                    peer = pair * 2 + core
                    send(y_ref.at[pl.ds(pl.multiple_of(peer * TALL, TALL), TALL), :], tall_k.at[col],
                         t_send.at[k], t_recv.at[k], {"col": peer})

            return carry

        lax.fori_loop(0, 4, tall_pair, 0)
        peer = col + 1 - 2 * (col % 2)
        send(y_ref.at[pl.ds(pl.multiple_of(peer * TALL, TALL), TALL), :], tall_k.at[col],
             t_send.at[k], t_recv.at[k], {"col": peer})
        tall_k[col] = y_ref[mine, :]

        @pl.when(k > 0)
        def _():
            sum_row(last_wide)

        wait(tall_k.at[pl.ds(0, NCOL - 1)], t_recv.at[k])
        panel = jnp.sum(tall_k[...], axis=0)
        own[pl.ds(0, TALL), :] = panel
        g_ref[first_tall] = gram_of(panel)
        sum_start(first_tall)
        wait(tall_k.at[pl.ds(0, NCOL - 1)], t_send.at[k])
        whole = tall_all.at[k]
        whole[mine, :] = panel

        @pl.when(k > 0)
        def _():
            sum_col(last_wide)

        sum_row(first_tall)
        for d in range(1, NCOL):
            send(whole.at[mine, :], whole.at[mine, :], ta_send.at[k], ta_recv.at[k],
                 {"col": (col + d) % NCOL})

        @pl.when(k > 0)
        def _():
            second_pass(last_wide)

        sum_col(first_tall)
        sum_end(first_tall)
        first_pass(first_tall, TALL, second_tall)
        wait(whole.at[pl.ds(0, TALL * (NCOL - 1)), :], ta_recv.at[k])

        def make_basis(t, carry):
            at = pl.ds(pl.multiple_of(t * 256, 256), 256)
            basis = mm(whole[at, :], total_ref[...])
            basis_ref[at, :] = basis
            b16[at, :] = basis.astype(bf16)
            return carry

        lax.fori_loop(0, ROWS // 256, make_basis, 0)
        wait(whole.at[pl.ds(0, TALL * (NCOL - 1)), :], ta_send.at[k])

        buffers = (rb0.at[k], rb1.at[k], rb2.at[k], rb3.at[k])
        start = [PART * q for q in range(4)]

        def times(at):
            part[at, :] = lax.dot_general(
                w_ref[:, at], b16[...], (((0,), (0,)), ((), ())), preferred_element_type=f32
            )

        def rows_at(offset, size):
            return pl.ds(pl.multiple_of(offset, PIECE), size)

        size = PART
        for s in range(4):
            size = size // 2
            for q in range(4):
                kind = ORDER[q][s]
                at = rows_at(start[q] + (1 - bit[kind]) * size, size)
                if s == 0:
                    at = pl.ds(pl.multiple_of(start[q] + (1 - bit[kind]) * size, 128), size)
                    times(at)
                send(part.at[at, :], buffers[s].at[q], r_send.at[k, s, q], r_recv.at[k, s, q],
                     {"row": partner[kind]})
            for q in range(4):
                kind = ORDER[q][s]
                start[q] = start[q] + bit[kind] * size
                if s == 0:
                    times(pl.ds(pl.multiple_of(start[q], 128), size))
            if s == 0:
                sum_row(second_tall)
            if s == 1:
                sum_col(second_tall)
            if s == 2:
                second_pass(second_tall)
            for q in range(4):
                at = rows_at(start[q], size)
                wait(buffers[s].at[q], r_recv.at[k, s, q])
                part[at, :] = part[at, :] + buffers[s][q]
        wide_k = wide_all.at[k]
        for q in range(4):
            at = rows_at(start[q], PIECE)
            own[pl.ds(PIECE * q, PIECE), :] = part[at, :]
            wide_k[at, :] = part[at, :]

        place = [list(start)]
        for j in range(4):
            now = list(place[-1])
            for q in range(4):
                now[q] = now[q] - bit[ORDER[q][3 - j]] * (PIECE << j)
            place.append(now)

        def gather_start(j):
            for q in range(4):
                at = rows_at(place[j][q], PIECE << j)
                send(wide_k.at[at, :], wide_k.at[at, :], a_send.at[k, j, q], a_recv.at[k, j, q],
                     {"row": partner[ORDER[q][3 - j]]})

        def gather_wait(j):
            for q in range(4):
                ref = wide_k.at[pl.ds(0, PIECE << j), :]
                wait(ref, a_recv.at[k, j, q])
                wait(ref, a_send.at[k, j, q])

        gather_start(0)
        g_ref[first_wide] = gram_of(own[...])
        sum_start(first_wide)
        for s in range(4):
            for q in range(4):
                wait(buffers[s].at[q], r_send.at[k, s, q])
        sum_row(first_wide)
        gather_wait(0)
        gather_start(1)
        sum_col(first_wide)
        gather_wait(1)
        gather_start(2)
        sum_end(first_wide)

        @pl.when(k < POWER)
        def _():
            first_pass(first_wide, OWN, second_wide)
            gather_wait(2)
            gather_start(3)
            gather_wait(3)

            def make_factor(t, carry):
                at = pl.ds(pl.multiple_of(t * 512, 512), 512)
                fac[at, :] = mm(wide_k[at, :], total_ref[...]).astype(bf16)
                return carry

            lax.fori_loop(0, PAD // 512, make_factor, 0)

        @pl.when(k == POWER)
        def _():
            eye = eye_of()

            def newton(_, pair):
                upper, inverse = pair
                middle = 1.5 * eye - 0.5 * mm(inverse, upper)
                return mm(upper, middle), mm(middle, inverse)

            def sqrt_pair(matrix, hook):
                scale = jnp.sqrt(jnp.sum(matrix * matrix, keepdims=True))
                pair = (matrix / scale, eye)
                pair = lax.fori_loop(0, NS_ITERS // 3, newton, pair)
                hook()
                pair = lax.fori_loop(0, NS_ITERS - NS_ITERS // 3, newton, pair)
                root = jnp.sqrt(scale)
                return pair[0] * root, pair[1] / root

            def last_gather():
                gather_wait(2)
                gather_start(3)

            second = second_ref[...]
            half, _ = sqrt_pair(mm(mm(second, ar3[first_wide]), second.T), last_gather)
            quarter, inv_quarter = sqrt_pair(half, lambda: None)
            q_ref[...] = mm(second.T, quarter)
            iq_ref[...] = mm(inv_quarter, second)
            gather_wait(3)
            wide_ref[...] = wide_k[...]

        return carry

    lax.fori_loop(0, STEPS, step, 0)


def factors(weight, sketch):
    vmem = pl.BlockSpec(memory_space=pltpu.VMEM)
    dma = pltpu.SemaphoreType.DMA
    return pl.pallas_call(
        factors_kernel,
        name="factors",
        out_shape=(
            jax.ShapeDtypeStruct((ROWS, RANK), f32),
            jax.ShapeDtypeStruct((PAD, RANK), f32),
            jax.ShapeDtypeStruct((RANK, RANK), f32),
            jax.ShapeDtypeStruct((RANK, RANK), f32),
        ),
        in_specs=[pl.BlockSpec(memory_space=pl.ANY), vmem],
        out_specs=(vmem, vmem, vmem, vmem),
        scratch_shapes=[
            pltpu.VMEM((ROWS, PAD), bf16),
            pltpu.VMEM((PAD, RANK), bf16),
            pltpu.VMEM((ROWS, RANK), bf16),
            pltpu.VMEM((PAD, RANK), f32),
            pltpu.VMEM((STEPS, NCOL, TALL, RANK), f32),
            pltpu.VMEM((STEPS, ROWS, RANK), f32),
            pltpu.VMEM((STEPS, 4, PART // 2, RANK), f32),
            pltpu.VMEM((STEPS, 4, PART // 4, RANK), f32),
            pltpu.VMEM((STEPS, 4, PART // 8, RANK), f32),
            pltpu.VMEM((STEPS, 4, PART // 16, RANK), f32),
            pltpu.VMEM((STEPS, PAD, RANK), f32),
            pltpu.VMEM((OWN, RANK), f32),
            pltpu.VMEM((STEPS * 4, RANK, RANK), f32),
            pltpu.VMEM((STEPS * 4, NCOL, SEG, RANK), f32),
            pltpu.VMEM((STEPS * 4, NROW, SEG, RANK), f32),
            pltpu.VMEM((STEPS * 4, RANK, RANK), f32),
            pltpu.VMEM((RANK, 2 * RANK), f32),
            pltpu.VMEM((RANK, RANK), f32),
            pltpu.VMEM((RANK, RANK), f32),
            pltpu.VMEM((RANK, RANK), f32),
            pltpu.VMEM((ROWS, RANK), f32),
            dma((4,)),
            dma((STEPS * 4, 3)),
            dma((STEPS * 4, 3)),
            dma((STEPS,)),
            dma((STEPS,)),
            dma((STEPS,)),
            dma((STEPS,)),
            dma((STEPS, 4, 4)),
            dma((STEPS, 4, 4)),
            dma((STEPS, 4, 4)),
            dma((STEPS, 4, 4)),
        ],
        compiler_params=pltpu.CompilerParams(
            collective_id=0, has_side_effects=True, vmem_limit_bytes=60 << 20
        ),
    )(weight, sketch)


def residual_kernel(w_ref, basis_ref, q_ref, iq_ref, wide_ref, fa_ref, fb_ref, res_ref, left):
    @pl.when(pl.program_id(0) == 0)
    def _():
        for t in range(ROWS // 256):
            at = pl.ds(t * 256, 256)
            a = mm(basis_ref[at, :], q_ref[...])
            fa_ref[at, :] = a
            hi = a.astype(bf16)
            low = (a - hi.astype(f32)).astype(bf16)
            left[at, :] = jnp.concatenate([hi, low, hi, low], 1)

    b = mm(iq_ref[...], wide_ref[...].T)
    fb_ref[...] = b
    hi = b.astype(bf16)
    low = (b - hi.astype(f32)).astype(bf16)
    product = jnp.dot(left[...], jnp.concatenate([hi, hi, low, low], 0), preferred_element_type=f32)
    res_ref[...] = (w_ref[...].astype(f32) - product).astype(bf16)


def residual(weight, basis, quarter, inv_quarter, wide):
    small = pl.BlockSpec((RANK, RANK), lambda i: (0, 0))
    panel = pl.BlockSpec((ROWS, RANK), lambda i: (0, 0))
    block = pl.BlockSpec((ROWS, TILE), lambda i: (0, i))
    return pl.pallas_call(
        residual_kernel,
        name="residual",
        grid=(COLS // TILE,),
        out_shape=(
            jax.ShapeDtypeStruct((ROWS, RANK), f32),
            jax.ShapeDtypeStruct((RANK, COLS), f32),
            jax.ShapeDtypeStruct((ROWS, COLS), bf16),
        ),
        in_specs=[block, panel, small, small, pl.BlockSpec((TILE, RANK), lambda i: (i, 0))],
        out_specs=(panel, pl.BlockSpec((RANK, TILE), lambda i: (0, i)), block),
        scratch_shapes=[pltpu.VMEM((ROWS, 4 * RANK), bf16)],
        compiler_params=pltpu.CompilerParams(vmem_limit_bytes=60 << 20),
    )(weight, basis, quarter, inv_quarter, wide)


def on_device(weight, sketch):
    basis, wide, quarter, inv_quarter = factors(weight, sketch)
    return residual(weight, basis, quarter, inv_quarter, wide)


def solution(mesh):
    return jax.shard_map(
        on_device,
        mesh=mesh,
        in_specs=(P("row", "col"), P("col", None)),
        out_specs=(P("row", None), P(None, "col"), P("row", "col")),
        check_vma=False,
    )
```

```python
import jax
import jax.numpy as jnp
from jax import lax
from jax.experimental import pallas as pl
from jax.experimental.pallas import tpu as pltpu
from jax.sharding import PartitionSpec as P

POWER = 2
NS_ITERS = 12
RANK = 128
ROWS = 1024
COLS = 4992
PAD = 5120
NCOL = 8
NROW = 16
PART = PAD // 4
OWN = PAD // NROW
PIECE = PART // NROW
TALL = ROWS // NCOL
SEG = RANK // NCOL
STEPS = POWER + 1
TILE = 384
BLOCK = 32
WIDE_TILES = 3
WIDE_TILE = COLS // WIDE_TILES

f32 = jnp.float32
bf16 = jnp.bfloat16
MESH = pl.DeviceIdType.MESH

ORDER = ((0, 2, 1, 3), (2, 1, 3, 0), (1, 3, 0, 2), (3, 0, 2, 1))


def split3(a):
    hi = a.astype(bf16)
    rest = a - hi.astype(f32)
    mid = rest.astype(bf16)
    low = (rest - mid.astype(f32)).astype(bf16)
    return hi, mid, low


def left6(a, axis):
    hi, mid, low = split3(a)
    return jnp.concatenate([hi, hi, mid, hi, low, mid], axis)


def right6(a, axis):
    hi, mid, low = split3(a)
    return jnp.concatenate([hi, mid, hi, low, hi, mid], axis)


def mm(a, b):
    return jnp.dot(left6(a, 1), right6(b, 0), preferred_element_type=f32)


def gram_of(y):
    return lax.dot_general(
        left6(y, 0), right6(y, 0), (((0,), (0,)), ((), ())), preferred_element_type=f32
    )


def eye_of():
    r = lax.broadcasted_iota(jnp.int32, (RANK, RANK), 0)
    c = lax.broadcasted_iota(jnp.int32, (RANK, RANK), 1)
    return jnp.where(r == c, 1.0, 0.0).astype(f32)


def newton_step(pair, eye):
    upper, inverse = pair
    middle = 1.5 * eye - 0.5 * mm(inverse, upper)
    return mm(upper, middle), mm(middle, inverse)


def cholesky_inverse(gram, s_ref, m_ref):
    s_ref[:, 0:RANK] = gram
    s_ref[:, RANK:] = eye_of()
    sub = lax.broadcasted_iota(jnp.int32, (8, RANK), 0)
    lane = lax.broadcasted_iota(jnp.int32, (BLOCK, RANK), 1)
    groups = range(BLOCK // 8)

    def spread(v, at):
        return jnp.broadcast_to(v[at : at + 1, :], (8, RANK))

    for o in range(0, RANK, BLOCK):
        u = [s_ref[o + 8 * g : o + 8 * g + 8, 0:RANK] for g in groups]
        n = [s_ref[o + 8 * g : o + 8 * g + 8, RANK:] for g in groups]
        square = [
            [jnp.broadcast_to(u[g][:, o + j : o + j + 1], (8, RANK)) if g >= j // 8 else None for g in groups]
            for j in range(BLOCK)
        ]
        scale = [jnp.ones((8, RANK), f32) for _ in groups]
        for j in range(BLOCK):
            top, at = divmod(j, 8)
            pivot = spread(square[j][top], at)
            inverse = 1.0 / pivot
            scale[top] = jnp.where(sub == at, lax.rsqrt(pivot), scale[top])
            u_row, n_row = spread(u[top], at), spread(n[top], at)
            times = {}
            for g in groups[top:]:
                column = square[j][g]
                if g == top:
                    column = jnp.where(sub > at, column, 0.0)
                times[g] = column * inverse
            for c in range(j + 1, BLOCK):
                entry = spread(square[j][c // 8], c % 8)
                for g in groups[c // 8 :]:
                    square[c][g] = square[c][g] - times[g] * entry
            for g in groups[top:]:
                u[g] = u[g] - times[g] * u_row
                n[g] = n[g] - times[g] * n_row
        u = jnp.concatenate([a * b for a, b in zip(u, scale)], 0)
        n = jnp.concatenate([a * b for a, b in zip(n, scale)], 0)
        m_ref[o : o + BLOCK, :] = n
        if o + BLOCK < RANK:
            u = jnp.where(lane >= o + BLOCK, u, 0.0)
            parts = []
            for v in (u, n):
                hi = v.astype(bf16).astype(f32)
                mid = (v - hi).astype(bf16).astype(f32)
                parts.append((hi, mid, v - hi - mid))
            (uh, um, ul), (nh, nm, nl) = parts
            left = jnp.concatenate([uh, uh, um, uh, ul, um], 0)
            right = jnp.concatenate(
                [
                    jnp.concatenate([uh, um, uh, ul, uh, um], 0),
                    jnp.concatenate([nh, nm, nh, nl, nh, nm], 0),
                ],
                1,
            )
            change = lax.dot_general(
                left, right, (((0,), (0,)), ((), ())), preferred_element_type=f32
            )
            s_ref[o + BLOCK :, :] = s_ref[o + BLOCK :, :] - change[o + BLOCK :, :]


def factors_kernel(
    w_hbm, sketch_ref, basis_ref, wide_ref, half_ref, total_ref,
    w_ref, fac, b16, part, tall_in, tall_all, rb0, rb1, rb2, rb3, wide_all,
    own, g_ref, ar1, ar2, ar3, s_ref, m_ref, tall_own, tall_first, tall_second, wide_second, y_ref,
    w_sem, ar_send, ar_recv, t_send, t_recv, ta_send, ta_recv, r_send, r_recv, a_send, a_recv,
):
    row = lax.axis_index("row")
    col = lax.axis_index("col")
    y = col // 2
    x = row // 4
    z = row % 4
    partner = ((x + 1 - 2 * (x % 2)) * 4 + z, (3 - x) * 4 + z, x * 4 + z + 1 - 2 * (z % 2), x * 4 + 3 - z)
    xhi, zhi = x // 2, z // 2
    bit = ((x + xhi) % 2, xhi, (z + zhi) % 2, zhi)

    def load(j):
        at = pl.ds(pl.multiple_of((y + 1 + j) % 4 * 2 * TALL, 2 * TALL), 2 * TALL)
        return pltpu.make_async_copy(w_hbm.at[at, :], w_ref.at[at, pl.ds(0, COLS)], w_sem.at[j])

    for j in range(4):
        load(j).start()

    barrier = pltpu.get_barrier_semaphore()
    for d in range(1, NCOL):
        pl.semaphore_signal(barrier, inc=1, device_id={"col": (col + d) % NCOL}, device_id_type=MESH)
    for d in range(1, NROW):
        pl.semaphore_signal(barrier, inc=1, device_id={"row": (row + d) % NROW}, device_id_type=MESH)

    w_ref[:, pl.ds(COLS, PAD - COLS)] = jnp.zeros((ROWS, PAD - COLS), bf16)
    fac[pl.ds(0, COLS), :] = sketch_ref[...]
    fac[pl.ds(COLS, PAD - COLS), :] = jnp.zeros((PAD - COLS, RANK), bf16)
    pl.semaphore_wait(barrier, NCOL + NROW - 2)

    def send(src, dst, send_sem, recv_sem, to):
        pltpu.make_async_remote_copy(
            src_ref=src, dst_ref=dst, send_sem=send_sem, recv_sem=recv_sem, device_id=to, device_id_type=MESH
        ).start()

    def wait(ref, sem):
        pltpu.make_async_copy(ref, ref, sem).wait()

    mine16 = pl.ds(pl.multiple_of(col * SEG, SEG), SEG)

    def sum_start(index):
        for d in range(1, NCOL):
            peer = (col + d) % NCOL
            send(g_ref.at[index, pl.ds(pl.multiple_of(peer * SEG, SEG), SEG), :], ar1.at[index, col],
                 ar_send.at[index, 0], ar_recv.at[index, 0], {"col": peer})
        ar1[index, col] = g_ref[index, mine16, :]

    def sum_row(index):
        wait(ar1.at[index, pl.ds(0, NCOL - 1)], ar_recv.at[index, 0])
        ar2[index, row] = jnp.sum(ar1[index], axis=0)
        for d in range(1, NROW):
            send(ar2.at[index, row], ar2.at[index, row], ar_send.at[index, 1], ar_recv.at[index, 1],
                 {"row": (row + d) % NROW})

    def sum_col(index):
        wait(ar2.at[index, pl.ds(0, NROW - 1)], ar_recv.at[index, 1])
        ar3[index, mine16, :] = jnp.sum(ar2[index], axis=0)
        for d in range(1, NCOL):
            send(ar3.at[index, mine16, :], ar3.at[index, mine16, :], ar_send.at[index, 2], ar_recv.at[index, 2],
                 {"col": (col + d) % NCOL})

    def sum_end(index):
        wait(ar3.at[index, pl.ds(0, SEG * (NCOL - 1)), :], ar_recv.at[index, 2])
        wait(ar1.at[index, pl.ds(0, NCOL - 1)], ar_send.at[index, 0])
        wait(ar2.at[index, pl.ds(0, NROW - 1)], ar_send.at[index, 1])
        wait(ar3.at[index, pl.ds(0, SEG * (NCOL - 1)), :], ar_send.at[index, 2])

    def corrected(index, before):
        return mm(mm(before, ar3[index]), before.T)

    wide_second[...] = eye_of()

    def step(k, carry):
        first_tall, second_tall, first_wide, second_wide = (k * 4 + i for i in range(4))
        last_wide = jnp.maximum(k - 1, 0) * 4 + 3

        mine = pl.ds(pl.multiple_of(col * TALL, TALL), TALL)
        tall_k = tall_in.at[k]

        def tall_pair(j, carry):
            pair = (y + 1 + j) % 4
            at = pl.ds(pl.multiple_of(pair * 2 * TALL, 2 * TALL), 2 * TALL)

            @pl.when(k == 0)
            def _():
                load(j).wait()

            y_ref[at, :] = jnp.dot(w_ref[at, :], fac[...], preferred_element_type=f32)

            @pl.when(j < 3)
            def _():
                for core in range(2):
                    peer = pair * 2 + core
                    send(y_ref.at[pl.ds(pl.multiple_of(peer * TALL, TALL), TALL), :], tall_k.at[col],
                         t_send.at[k], t_recv.at[k], {"col": peer})

            return carry

        lax.fori_loop(0, 4, tall_pair, 0)
        peer = col + 1 - 2 * (col % 2)
        send(y_ref.at[pl.ds(pl.multiple_of(peer * TALL, TALL), TALL), :], tall_k.at[col],
             t_send.at[k], t_recv.at[k], {"col": peer})
        tall_k[col] = y_ref[mine, :]

        @pl.when(k > 0)
        def _():
            sum_row(last_wide)

        wait(tall_k.at[pl.ds(0, NCOL - 1)], t_recv.at[k])
        panel = jnp.sum(tall_k[...], axis=0)
        whole = tall_all.at[k]
        whole[mine, :] = panel
        for d in range(1, NCOL):
            send(whole.at[mine, :], whole.at[mine, :], ta_send.at[k], ta_recv.at[k],
                 {"col": (col + d) % NCOL})
        tall_own[...] = panel
        g_ref[first_tall] = gram_of(panel)
        sum_start(first_tall)

        @pl.when(k > 0)
        def _():
            sum_col(last_wide)

        wait(whole.at[pl.ds(0, TALL * (NCOL - 1)), :], ta_recv.at[k])
        raw = whole[...]
        high = raw.astype(bf16)
        b16[:, 0:RANK] = high
        b16[:, RANK:] = (raw - high.astype(f32)).astype(bf16)

        buffers = (rb0.at[k], rb1.at[k], rb2.at[k], rb3.at[k])
        start = [PART * q for q in range(4)]

        def times(at):
            both = lax.dot_general(
                w_ref[:, at], b16[...], (((0,), (0,)), ((), ())), preferred_element_type=f32
            )
            part[at, :] = both[:, 0:RANK] + both[:, RANK:]

        def rows_at(offset, size):
            return pl.ds(pl.multiple_of(offset, PIECE), size)

        size = PART
        for s in range(3):
            size = size // 2
            for q in range(4):
                kind = ORDER[q][s]
                at = rows_at(start[q] + (1 - bit[kind]) * size, size)
                if s == 0:
                    at = pl.ds(pl.multiple_of(start[q] + (1 - bit[kind]) * size, 128), size)
                    times(at)
                send(part.at[at, :], buffers[s].at[q], r_send.at[k, s, q], r_recv.at[k, s, q],
                     {"row": partner[kind]})
            for q in range(4):
                kind = ORDER[q][s]
                start[q] = start[q] + bit[kind] * size
                if s == 0:
                    times(pl.ds(pl.multiple_of(start[q], 128), size))
            if s == 0:
                sum_row(first_tall)

                @pl.when(k > 0)
                def _():
                    sum_end(last_wide)
                    cholesky_inverse(ar3[last_wide], s_ref, wide_second)

            if s == 1:
                sum_col(first_tall)
            if s == 2:
                sum_end(first_tall)
                cholesky_inverse(corrected(first_tall, wide_second[...]), s_ref, m_ref)
                tall_first[...] = mm(m_ref[...], wide_second[...])
                g_ref[second_tall] = gram_of(mm(tall_own[...], tall_first[...].T))
                sum_start(second_tall)
            for q in range(4):
                at = rows_at(start[q], size)
                wait(buffers[s].at[q], r_recv.at[k, s, q])
                part[at, :] = part[at, :] + buffers[s][q]
        wide_k = wide_all.at[k]
        for q in range(4):
            send(part.at[rows_at(start[q], size), :], buffers[3].at[q], r_send.at[k, 3, q], r_recv.at[k, 3, q],
                 {"row": partner[ORDER[q][3]]})
        sum_row(second_tall)
        for q in range(4):
            at = rows_at(start[q], size)
            wait(buffers[3].at[q], r_recv.at[k, 3, q])
            wide_k[at, :] = part[at, :] + buffers[3][q]
        for q in range(4):
            at = rows_at(start[q] + bit[ORDER[q][3]] * PIECE, PIECE)
            own[pl.ds(PIECE * q, PIECE), :] = wide_k[at, :]

        place = [list(start)]
        for j in range(3):
            now = list(place[-1])
            for q in range(4):
                now[q] = now[q] - bit[ORDER[q][2 - j]] * (size << j)
            place.append(now)

        def gather_start(j):
            for q in range(4):
                at = rows_at(place[j][q], size << j)
                send(wide_k.at[at, :], wide_k.at[at, :], a_send.at[k, j, q], a_recv.at[k, j, q],
                     {"row": partner[ORDER[q][2 - j]]})

        def gather_wait(j):
            for q in range(4):
                ref = wide_k.at[pl.ds(0, size << j), :]
                wait(ref, a_recv.at[k, j, q])
                wait(ref, a_send.at[k, j, q])

        gather_start(0)
        own[...] = mm(own[...], tall_first[...].T)
        g_ref[first_wide] = gram_of(own[...])
        sum_start(first_wide)
        wait(tall_k.at[pl.ds(0, NCOL - 1)], t_send.at[k])
        wait(whole.at[pl.ds(0, TALL * (NCOL - 1)), :], ta_send.at[k])
        for s in range(4):
            for q in range(4):
                wait(buffers[s].at[q], r_send.at[k, s, q])
        sum_col(second_tall)
        sum_row(first_wide)
        gather_wait(0)
        gather_start(1)
        sum_end(second_tall)
        cholesky_inverse(ar3[second_tall], s_ref, tall_second)
        sum_col(first_wide)
        gather_wait(1)
        gather_start(2)
        second = tall_second[...]
        total = mm(second, tall_first[...])
        sum_end(first_wide)
        gram = corrected(first_wide, second)

        @pl.when(k < POWER)
        def _():
            cholesky_inverse(gram, s_ref, m_ref)
            inverse = m_ref[...]
            turned = mm(inverse, total).T
            g_ref[second_wide] = gram_of(mm(own[...], mm(inverse, second).T))
            sum_start(second_wide)
            gather_wait(2)
            right = right6(turned, 0)

            def make_factor(t, carry):
                at = pl.ds(pl.multiple_of(t * 512, 512), 512)
                fac[at, :] = jnp.dot(left6(wide_k[at, :], 1), right, preferred_element_type=f32).astype(bf16)
                return carry

            lax.fori_loop(0, PAD // 512, make_factor, 0)

        @pl.when(k == POWER)
        def _():
            eye = eye_of()
            scale = jnp.sqrt(jnp.sum(gram * gram, keepdims=True))

            def newton(_, pair):
                return newton_step(pair, eye)

            pair = lax.fori_loop(0, NS_ITERS, newton, (gram / scale, eye))
            half_ref[...] = pair[0] * jnp.sqrt(scale)
            total_ref[...] = total
            basis_ref[...] = whole[...]
            gather_wait(2)
            wide_ref[...] = wide_k[...]

        return carry

    lax.fori_loop(0, STEPS, step, 0)


def factors(weight, sketch):
    vmem = pl.BlockSpec(memory_space=pltpu.VMEM)
    dma = pltpu.SemaphoreType.DMA
    return pl.pallas_call(
        factors_kernel,
        name="factors",
        out_shape=(
            jax.ShapeDtypeStruct((ROWS, RANK), f32),
            jax.ShapeDtypeStruct((PAD, RANK), f32),
            jax.ShapeDtypeStruct((RANK, RANK), f32),
            jax.ShapeDtypeStruct((RANK, RANK), f32),
        ),
        in_specs=[pl.BlockSpec(memory_space=pl.ANY), vmem],
        out_specs=(vmem, vmem, vmem, vmem),
        scratch_shapes=[
            pltpu.VMEM((ROWS, PAD), bf16),
            pltpu.VMEM((PAD, RANK), bf16),
            pltpu.VMEM((ROWS, 2 * RANK), bf16),
            pltpu.VMEM((PAD, RANK), f32),
            pltpu.VMEM((STEPS, NCOL, TALL, RANK), f32),
            pltpu.VMEM((STEPS, ROWS, RANK), f32),
            pltpu.VMEM((STEPS, 4, PART // 2, RANK), f32),
            pltpu.VMEM((STEPS, 4, PART // 4, RANK), f32),
            pltpu.VMEM((STEPS, 4, PART // 8, RANK), f32),
            pltpu.VMEM((STEPS, 4, PART // 8, RANK), f32),
            pltpu.VMEM((STEPS, PAD, RANK), f32),
            pltpu.VMEM((OWN, RANK), f32),
            pltpu.VMEM((STEPS * 4, RANK, RANK), f32),
            pltpu.VMEM((STEPS * 4, NCOL, SEG, RANK), f32),
            pltpu.VMEM((STEPS * 4, NROW, SEG, RANK), f32),
            pltpu.VMEM((STEPS * 4, RANK, RANK), f32),
            pltpu.VMEM((RANK, 2 * RANK), f32),
            pltpu.VMEM((RANK, RANK), f32),
            pltpu.VMEM((TALL, RANK), f32),
            pltpu.VMEM((RANK, RANK), f32),
            pltpu.VMEM((RANK, RANK), f32),
            pltpu.VMEM((RANK, RANK), f32),
            pltpu.VMEM((ROWS, RANK), f32),
            dma((4,)),
            dma((STEPS * 4, 3)),
            dma((STEPS * 4, 3)),
            dma((STEPS,)),
            dma((STEPS,)),
            dma((STEPS,)),
            dma((STEPS,)),
            dma((STEPS, 4, 4)),
            dma((STEPS, 4, 4)),
            dma((STEPS, 3, 4)),
            dma((STEPS, 3, 4)),
        ],
        compiler_params=pltpu.CompilerParams(
            collective_id=0, has_side_effects=True, vmem_limit_bytes=60 << 20
        ),
    )(weight, sketch)


def residual_kernel(
    w_hbm, basis_hbm, wide_hbm, half_ref, total_ref, fa_hbm, fb_hbm, res_hbm,
    w_ref, basis_ref, wide_ref, six, left, right, fa_ref, fb_ref, w_sem, in_sem, fa_sem, fb_sem, res_sem,
):
    wide_load = pltpu.make_async_copy(wide_hbm, wide_ref, in_sem.at[0])
    basis_load = pltpu.make_async_copy(basis_hbm, basis_ref, in_sem.at[1])
    wide_load.start()
    basis_load.start()
    loads = []
    for i in range(4):
        at = pl.ds(i * 256, 256)
        loads.append(pltpu.make_async_copy(w_hbm.at[at, :], w_ref.at[at, :], w_sem.at[i]))
        loads[-1].start()
    wide_load.wait()

    def prepare(t):
        at = pl.ds(pl.multiple_of(t * TILE, 128), TILE)
        six[:, at] = right6(wide_ref[at, :].T, 0)

    eye = eye_of()
    half = half_ref[...]
    scale = jnp.sqrt(jnp.sum(half * half, keepdims=True))

    def newton(i, pair):
        prepare(i)
        return newton_step(pair, eye)

    upper, inverse = lax.fori_loop(0, NS_ITERS, newton, (half / scale, eye))
    prepare(NS_ITERS)
    root = jnp.sqrt(scale)
    total = total_ref[...]
    quarter = mm(total.T, upper * root)
    six_left = left6(mm(inverse / root, total), 1)
    basis_load.wait()
    fa_store = pltpu.make_async_copy(fa_ref, fa_hbm, fa_sem)
    for t in range(ROWS // 256):
        at = pl.ds(t * 256, 256)
        a = mm(basis_ref[at, :], quarter)
        fa_ref[at, :] = a
        hi = a.astype(bf16)
        low = (a - hi.astype(f32)).astype(bf16)
        left[at, :] = jnp.concatenate([hi, low, hi], 1)
    fa_store.start()
    stores = [fa_store]
    for load in loads:
        load.wait()
    for t in range(WIDE_TILES):
        at = pl.ds(t * WIDE_TILE, WIDE_TILE)
        b = jnp.dot(six_left, six[:, at], preferred_element_type=f32)
        fb_ref[:, at] = b
        hi = b.astype(bf16)
        low = (b - hi.astype(f32)).astype(bf16)
        right[:, at] = jnp.concatenate([hi, hi, low], 0)
        stores.append(pltpu.make_async_copy(fb_ref.at[:, at], fb_hbm.at[:, at], fb_sem.at[t]))
        stores[-1].start()
        for r in range(2):
            rows = pl.ds(r * (ROWS // 2), ROWS // 2)
            product = jnp.dot(left[rows, :], right[:, at], preferred_element_type=f32)
            w_ref[rows, at] = (w_ref[rows, at].astype(f32) - product).astype(bf16)
            stores.append(pltpu.make_async_copy(w_ref.at[rows, at], res_hbm.at[rows, at], res_sem.at[t, r]))
            stores[-1].start()
    for store in stores:
        store.wait()


def residual(weight, basis, wide, half, total):
    vmem = pl.BlockSpec(memory_space=pltpu.VMEM)
    hbm = pl.BlockSpec(memory_space=pl.ANY)
    dma = pltpu.SemaphoreType.DMA
    return pl.pallas_call(
        residual_kernel,
        name="residual",
        out_shape=(
            jax.ShapeDtypeStruct((ROWS, RANK), f32),
            jax.ShapeDtypeStruct((RANK, COLS), f32),
            jax.ShapeDtypeStruct((ROWS, COLS), bf16),
        ),
        in_specs=[hbm, hbm, hbm, vmem, vmem],
        out_specs=(hbm, hbm, hbm),
        scratch_shapes=[
            pltpu.VMEM((ROWS, COLS), bf16),
            pltpu.VMEM((ROWS, RANK), f32),
            pltpu.VMEM((PAD, RANK), f32),
            pltpu.VMEM((6 * RANK, COLS), bf16),
            pltpu.VMEM((ROWS, 3 * RANK), bf16),
            pltpu.VMEM((3 * RANK, COLS), bf16),
            pltpu.VMEM((ROWS, RANK), f32),
            pltpu.VMEM((RANK, COLS), f32),
            dma((4,)),
            dma((2,)),
            dma,
            dma((WIDE_TILES,)),
            dma((WIDE_TILES, 2)),
        ],
        compiler_params=pltpu.CompilerParams(vmem_limit_bytes=60 << 20),
    )(weight, basis, wide, half, total)


def on_device(weight, sketch):
    return residual(weight, *factors(weight, sketch))


def solution(mesh):
    return jax.shard_map(
        on_device,
        mesh=mesh,
        in_specs=(P("row", "col"), P("col", None)),
        out_specs=(P("row", None), P(None, "col"), P("row", "col")),
        check_vma=False,
    )
```

```python
import jax
import jax.numpy as jnp
from jax import lax
from jax.experimental import pallas as pl
from jax.experimental.pallas import tpu as pltpu
from jax.sharding import PartitionSpec as P

POWER = 2
NS_ITERS = 12
RANK = 128
ROWS = 1024
COLS = 4992
PAD = 5120
NCOL = 8
NROW = 16
PART = PAD // 4
OWN = PAD // NROW
PIECE = PART // NROW
TALL = ROWS // NCOL
SEG = RANK // NCOL
STEPS = POWER + 1
TILE = 384
BLOCK = 32
WIDE_TILES = 3
WIDE_TILE = COLS // WIDE_TILES

f32 = jnp.float32
bf16 = jnp.bfloat16
MESH = pl.DeviceIdType.MESH

ORDER = ((0, 2, 1, 3), (2, 1, 3, 0), (1, 3, 0, 2), (3, 0, 2, 1))

MESSAGES = ((0, 320), (320, 320), (640, 160), (800, 160), (960, 160), (1120, 160))
LOW_FROM = (POWER, POWER, POWER, POWER, 0, 0)
GATHER = (2, 1, 0, 1, 0, 0)


def split3(a):
    hi = a.astype(bf16)
    rest = a - hi.astype(f32)
    mid = rest.astype(bf16)
    low = (rest - mid.astype(f32)).astype(bf16)
    return hi, mid, low


def left6(a, axis):
    hi, mid, low = split3(a)
    return jnp.concatenate([hi, hi, mid, hi, low, mid], axis)


def right6(a, axis):
    hi, mid, low = split3(a)
    return jnp.concatenate([hi, mid, hi, low, hi, mid], axis)


def mm(a, b):
    return jnp.dot(left6(a, 1), right6(b, 0), preferred_element_type=f32)


def gram_of(y):
    return lax.dot_general(
        left6(y, 0), right6(y, 0), (((0,), (0,)), ((), ())), preferred_element_type=f32
    )


def eye_of():
    r = lax.broadcasted_iota(jnp.int32, (RANK, RANK), 0)
    c = lax.broadcasted_iota(jnp.int32, (RANK, RANK), 1)
    return jnp.where(r == c, 1.0, 0.0).astype(f32)


def newton_step(pair, eye):
    upper, inverse = pair
    middle = 1.5 * eye - 0.5 * mm(inverse, upper)
    return mm(upper, middle), mm(middle, inverse)


def cholesky_inverse(gram, s_ref, m_ref):
    s_ref[:, 0:RANK] = gram
    s_ref[:, RANK:] = eye_of()
    sub = lax.broadcasted_iota(jnp.int32, (8, RANK), 0)
    lane = lax.broadcasted_iota(jnp.int32, (BLOCK, RANK), 1)
    groups = range(BLOCK // 8)

    def spread(v, at):
        return jnp.broadcast_to(v[at : at + 1, :], (8, RANK))

    for o in range(0, RANK, BLOCK):
        u = [s_ref[o + 8 * g : o + 8 * g + 8, 0:RANK] for g in groups]
        n = [s_ref[o + 8 * g : o + 8 * g + 8, RANK:] for g in groups]
        square = [
            [jnp.broadcast_to(u[g][:, o + j : o + j + 1], (8, RANK)) if g >= j // 8 else None for g in groups]
            for j in range(BLOCK)
        ]
        scale = [jnp.ones((8, RANK), f32) for _ in groups]
        for j in range(BLOCK):
            top, at = divmod(j, 8)
            pivot = spread(square[j][top], at)
            inverse = 1.0 / pivot
            scale[top] = jnp.where(sub == at, lax.rsqrt(pivot), scale[top])
            u_row, n_row = spread(u[top], at), spread(n[top], at)
            times = {}
            for g in groups[top:]:
                column = square[j][g]
                if g == top:
                    column = jnp.where(sub > at, column, 0.0)
                times[g] = column * inverse
            for c in range(j + 1, BLOCK):
                entry = spread(square[j][c // 8], c % 8)
                for g in groups[c // 8 :]:
                    square[c][g] = square[c][g] - times[g] * entry
            for g in groups[top:]:
                u[g] = u[g] - times[g] * u_row
                n[g] = n[g] - times[g] * n_row
        u = jnp.concatenate([a * b for a, b in zip(u, scale)], 0)
        n = jnp.concatenate([a * b for a, b in zip(n, scale)], 0)
        m_ref[o : o + BLOCK, :] = n
        if o + BLOCK < RANK:
            u = jnp.where(lane >= o + BLOCK, u, 0.0)
            parts = []
            for v in (u, n):
                hi = v.astype(bf16).astype(f32)
                mid = (v - hi).astype(bf16).astype(f32)
                parts.append((hi, mid, v - hi - mid))
            (uh, um, ul), (nh, nm, nl) = parts
            left = jnp.concatenate([uh, uh, um, uh, ul, um], 0)
            right = jnp.concatenate(
                [
                    jnp.concatenate([uh, um, uh, ul, uh, um], 0),
                    jnp.concatenate([nh, nm, nh, nl, nh, nm], 0),
                ],
                1,
            )
            change = lax.dot_general(
                left, right, (((0,), (0,)), ((), ())), preferred_element_type=f32
            )
            s_ref[o + BLOCK :, :] = s_ref[o + BLOCK :, :] - change[o + BLOCK :, :]


def factors_kernel(
    w_hbm, sketch_ref, basis_ref, wide_ref, half_ref, total_ref,
    w_ref, fac, b16, part, core_in, core_sum, tall_in, tall_all, stage_hi, stage_lo, land_hi, land_lo, wide_all,
    own, g_ref, ar1, ar2, ar3, s_ref, m_ref, tall_own, tall_first, tall_second, wide_second, y_ref,
    w_sem, ar_send, ar_recv, c_send, c_recv, t_send, t_recv, ta_send, ta_recv, r_send, r_recv, l_send, l_recv, a_send, a_recv,
):
    row = lax.axis_index("row")
    col = lax.axis_index("col")
    y = col // 2
    x = row // 4
    z = row % 4
    partner = ((x + 1 - 2 * (x % 2)) * 4 + z, (3 - x) * 4 + z, x * 4 + z + 1 - 2 * (z % 2), x * 4 + 3 - z)
    xhi, zhi = x // 2, z // 2
    bit = ((x + xhi) % 2, xhi, (z + zhi) % 2, zhi)

    def load(j):
        at = pl.ds(pl.multiple_of((y + 1 + j) % 4 * 2 * TALL, 2 * TALL), 2 * TALL)
        return pltpu.make_async_copy(w_hbm.at[at, :], w_ref.at[at, pl.ds(0, COLS)], w_sem.at[j])

    for j in range(4):
        load(j).start()

    barrier = pltpu.get_barrier_semaphore()
    for d in range(1, NCOL):
        pl.semaphore_signal(barrier, inc=1, device_id={"col": (col + d) % NCOL}, device_id_type=MESH)
    for d in range(1, NROW):
        pl.semaphore_signal(barrier, inc=1, device_id={"row": (row + d) % NROW}, device_id_type=MESH)

    w_ref[:, pl.ds(COLS, PAD - COLS)] = jnp.zeros((ROWS, PAD - COLS), bf16)
    fac[pl.ds(0, COLS), :] = sketch_ref[...]
    fac[pl.ds(COLS, PAD - COLS), :] = jnp.zeros((PAD - COLS, RANK), bf16)
    pl.semaphore_wait(barrier, NCOL + NROW - 2)

    def send(src, dst, send_sem, recv_sem, to):
        pltpu.make_async_remote_copy(
            src_ref=src, dst_ref=dst, send_sem=send_sem, recv_sem=recv_sem, device_id=to, device_id_type=MESH
        ).start()

    def wait(ref, sem):
        pltpu.make_async_copy(ref, ref, sem).wait()

    mine16 = pl.ds(pl.multiple_of(col * SEG, SEG), SEG)

    def sum_start(index):
        for d in range(1, NCOL):
            peer = (col + d) % NCOL
            send(g_ref.at[index, pl.ds(pl.multiple_of(peer * SEG, SEG), SEG), :], ar1.at[index, col],
                 ar_send.at[index, 0], ar_recv.at[index, 0], {"col": peer})
        ar1[index, col] = g_ref[index, mine16, :]

    def sum_row(index):
        wait(ar1.at[index, pl.ds(0, NCOL - 1)], ar_recv.at[index, 0])
        ar2[index, row] = jnp.sum(ar1[index], axis=0)
        for d in range(1, NROW):
            send(ar2.at[index, row], ar2.at[index, row], ar_send.at[index, 1], ar_recv.at[index, 1],
                 {"row": (row + d) % NROW})

    def sum_col(index):
        wait(ar2.at[index, pl.ds(0, NROW - 1)], ar_recv.at[index, 1])
        ar3[index, mine16, :] = jnp.sum(ar2[index], axis=0)
        for d in range(1, NCOL):
            send(ar3.at[index, mine16, :], ar3.at[index, mine16, :], ar_send.at[index, 2], ar_recv.at[index, 2],
                 {"col": (col + d) % NCOL})

    def sum_end(index):
        wait(ar3.at[index, pl.ds(0, SEG * (NCOL - 1)), :], ar_recv.at[index, 2])
        wait(ar1.at[index, pl.ds(0, NCOL - 1)], ar_send.at[index, 0])
        wait(ar2.at[index, pl.ds(0, NROW - 1)], ar_send.at[index, 1])
        wait(ar3.at[index, pl.ds(0, SEG * (NCOL - 1)), :], ar_send.at[index, 2])

    def corrected(index, before):
        return mm(mm(before, ar3[index]), before.T)

    wide_second[...] = eye_of()

    def step(k, carry):
        first_tall, second_tall, first_wide, second_wide = (k * 4 + i for i in range(4))
        last_wide = jnp.maximum(k - 1, 0) * 4 + 3

        mine = pl.ds(pl.multiple_of(col * TALL, TALL), TALL)
        tall_k = tall_in.at[k]

        core = col % 2
        sibling = {"col": col + 1 - 2 * core}

        def chunk(index):
            return pl.ds(pl.multiple_of(index * TALL, TALL), TALL)

        def tall_pair(j, carry):
            pair = (y + 1 + j) % 4
            at = pl.ds(pl.multiple_of(pair * 2 * TALL, 2 * TALL), 2 * TALL)

            @pl.when(k == 0)
            def _():
                load(j).wait()

            y_ref[at, :] = jnp.dot(w_ref[at, :], fac[...], preferred_element_type=f32)
            send(y_ref.at[chunk(pair * 2 + 1 - core), :], core_in.at[k, j], c_send.at[k, j], c_recv.at[k, j], sibling)

            @pl.when(j > 0)
            def _():
                before = (y + j) % 4 * 2 + core
                wait(core_in.at[k, j - 1], c_recv.at[k, j - 1])
                core_sum[j - 1] = y_ref[chunk(before), :] + core_in[k, j - 1]
                send(core_sum.at[j - 1], tall_k.at[y], t_send.at[k], t_recv.at[k], {"col": before})

            return carry

        lax.fori_loop(0, 4, tall_pair, 0)
        wait(core_in.at[k, 3], c_recv.at[k, 3])
        tall_k[y] = y_ref[mine, :] + core_in[k, 3]

        @pl.when(k > 0)
        def _():
            sum_row(last_wide)

        wait(tall_k.at[pl.ds(0, 3)], t_recv.at[k])
        panel = jnp.sum(tall_k[...], axis=0)
        whole = tall_all.at[k]
        whole[mine, :] = panel
        for d in (1, 3, 2):
            send(whole.at[mine, :], whole.at[mine, :], ta_send.at[k, 4 - d], ta_recv.at[k, 4 - d],
                 {"col": (y + d) % 4 * 2 + core})
        send(whole.at[mine, :], whole.at[mine, :], ta_send.at[k, 0], ta_recv.at[k, 0], sibling)
        tall_own[...] = panel
        g_ref[first_tall] = gram_of(panel)
        sum_start(first_tall)

        @pl.when(k > 0)
        def _():
            sum_col(last_wide)

        for d in (1, 3, 2):
            at = chunk((y + d) % 4 * 2 + core)
            wait(whole.at[at, :], ta_recv.at[k, d])
            send(whole.at[at, :], whole.at[at, :], ta_send.at[k, 4 + d], ta_recv.at[k, 4 + d], sibling)
        for d in (0, 5, 6, 7):
            wait(whole.at[mine, :], ta_recv.at[k, d])
        sum_row(first_tall)
        raw = whole[...]
        high = raw.astype(bf16)
        b16[:, 0:RANK] = high
        b16[:, RANK:] = (raw - high.astype(f32)).astype(bf16)

        def times(at):
            both = lax.dot_general(
                w_ref[:, at], b16[...], (((0,), (0,)), ((), ())), preferred_element_type=f32
            )
            part[at, :] = both[:, 0:RANK] + both[:, RANK:]

        def rows_at(offset, size):
            return pl.ds(pl.multiple_of(offset, PIECE), size)

        def post(m, q, kind, offset):
            start, size = MESSAGES[m]
            at = rows_at(offset, size)
            land = pl.ds(start, size)
            value = part[at, :]
            high = value.astype(bf16)
            stage_hi[at, :] = high
            send(stage_hi.at[at, :], land_hi.at[k, q, land, :], r_send.at[k, m, q], r_recv.at[k, m, q],
                 {"row": partner[kind]})

            @pl.when(k >= LOW_FROM[m])
            def _():
                stage_lo[at, :] = (value - high.astype(f32)).astype(bf16)
                send(stage_lo.at[at, :], land_lo.at[k, q, land, :], l_send.at[k, m, q], l_recv.at[k, m, q],
                     {"row": partner[kind]})

        def take(m, q, offset):
            start, size = MESSAGES[m]
            at = rows_at(offset, size)
            land = pl.ds(start, size)
            wait(land_hi.at[k, q, land, :], r_recv.at[k, m, q])
            part[at, :] = part[at, :] + land_hi[k, q, land, :].astype(f32)

            @pl.when(k >= LOW_FROM[m])
            def _():
                wait(land_lo.at[k, q, land, :], l_recv.at[k, m, q])
                part[at, :] = part[at, :] + land_lo[k, q, land, :].astype(f32)

        kinds = ORDER
        half_size, quarter_size, size = PART // 2, PART // 4, PART // 8
        keep0, keep1, send1, keep2, send2 = [], [], [], [], []
        for q in range(4):
            b0, b1, b2 = (bit[kinds[q][s]] for s in range(3))
            away = PART * q + (1 - b0) * half_size
            times(pl.ds(pl.multiple_of(away, 128), half_size))
            post(0, q, kinds[q][0], away + (1 - b1) * quarter_size)
            post(1, q, kinds[q][0], away + b1 * quarter_size)
            keep0.append(PART * q + b0 * half_size)
            send1.append(keep0[q] + (1 - b1) * quarter_size)
            keep1.append(keep0[q] + b1 * quarter_size)
            send2.append(keep1[q] + (1 - b2) * size)
            keep2.append(keep1[q] + b2 * size)
        for q in range(4):
            times(pl.ds(pl.multiple_of(keep0[q], 128), half_size))

        @pl.when(k > 0)
        def _():
            sum_end(last_wide)
            cholesky_inverse(ar3[last_wide], s_ref, wide_second)

        for q in range(4):
            b2 = bit[kinds[q][2]]
            take(0, q, send1[q])
            post(2, q, kinds[q][1], send1[q] + (1 - b2) * size)
            post(3, q, kinds[q][1], send1[q] + b2 * size)
        sum_col(first_tall)
        for q in range(4):
            take(1, q, keep1[q])
        for q in range(4):
            take(2, q, send2[q])
            post(4, q, kinds[q][2], send2[q])
        sum_end(first_tall)
        cholesky_inverse(corrected(first_tall, wide_second[...]), s_ref, m_ref)
        for q in range(4):
            take(3, q, keep2[q])
        for q in range(4):
            take(4, q, keep2[q])
            post(5, q, kinds[q][3], keep2[q])
        tall_first[...] = mm(m_ref[...], wide_second[...])
        g_ref[second_tall] = gram_of(mm(tall_own[...], tall_first[...].T))
        sum_start(second_tall)
        wide_k = wide_all.at[k]
        for q in range(4):
            at = rows_at(keep2[q], size)
            land = pl.ds(*MESSAGES[5])
            wait(land_hi.at[k, q, land, :], r_recv.at[k, 5, q])
            wide_k[at, :] = stage_hi[at, :].astype(f32) + land_hi[k, q, land, :].astype(f32)
            wait(land_lo.at[k, q, land, :], l_recv.at[k, 5, q])
            low = stage_lo[at, :].astype(f32) + land_lo[k, q, land, :].astype(f32)
            wide_k[at, :] = wide_k[at, :] + low

        for q in range(4):
            at = rows_at(keep2[q] + bit[kinds[q][3]] * PIECE, PIECE)
            own[pl.ds(PIECE * q, PIECE), :] = wide_k[at, :]

        def gather(g, offsets, rows):
            for q in range(4):
                at = rows_at(offsets[q], rows)
                send(wide_k.at[at, :], wide_k.at[at, :], a_send.at[k, g, q], a_recv.at[k, g, q],
                     {"row": partner[kinds[q][GATHER[g]]]})

        def gather_wait(g, rows, sem):
            for q in range(4):
                wait(wide_k.at[pl.ds(0, rows), :], sem.at[k, g, q])

        for g in range(3):
            gather(g, keep2, size)
        own[...] = mm(own[...], tall_first[...].T)
        g_ref[first_wide] = gram_of(own[...])
        sum_start(first_wide)
        sum_row(second_tall)
        wait(tall_k.at[pl.ds(0, 3)], t_send.at[k])
        for j in range(4):
            wait(core_in.at[k, j], c_send.at[k, j])
        for d in (0, 1, 2, 3, 5, 6, 7):
            wait(whole.at[mine, :], ta_send.at[k, d])
        for m, (_, rows) in enumerate(MESSAGES):
            for q in range(4):
                wait(stage_hi.at[pl.ds(0, rows), :], r_send.at[k, m, q])

                @pl.when(k >= LOW_FROM[m])
                def _():
                    wait(stage_lo.at[pl.ds(0, rows), :], l_send.at[k, m, q])

        sum_row(first_wide)
        gather_wait(0, size, a_recv)
        gather(3, send2, size)
        gather(4, send2, size)
        sum_col(second_tall)
        sum_col(first_wide)
        gather_wait(1, size, a_recv)
        gather_wait(3, size, a_recv)
        gather(5, send1, 2 * size)
        sum_end(second_tall)
        cholesky_inverse(ar3[second_tall], s_ref, tall_second)

        def gather_end():
            gather_wait(2, size, a_recv)
            gather_wait(4, size, a_recv)
            gather_wait(5, 2 * size, a_recv)
            for g in range(5):
                gather_wait(g, size, a_send)
            gather_wait(5, 2 * size, a_send)

        second = tall_second[...]
        total = mm(second, tall_first[...])
        sum_end(first_wide)
        gram = corrected(first_wide, second)

        @pl.when(k < POWER)
        def _():
            cholesky_inverse(gram, s_ref, m_ref)
            inverse = m_ref[...]
            turned = mm(inverse, total).T
            g_ref[second_wide] = gram_of(mm(own[...], mm(inverse, second).T))
            sum_start(second_wide)
            gather_end()
            right = right6(turned, 0)

            def make_factor(t, carry):
                at = pl.ds(pl.multiple_of(t * 512, 512), 512)
                fac[at, :] = jnp.dot(left6(wide_k[at, :], 1), right, preferred_element_type=f32).astype(bf16)
                return carry

            lax.fori_loop(0, PAD // 512, make_factor, 0)

        @pl.when(k == POWER)
        def _():
            eye = eye_of()
            scale = jnp.sqrt(jnp.sum(gram * gram, keepdims=True))

            def newton(_, pair):
                return newton_step(pair, eye)

            pair = lax.fori_loop(0, NS_ITERS, newton, (gram / scale, eye))
            half_ref[...] = pair[0] * jnp.sqrt(scale)
            total_ref[...] = total
            basis_ref[...] = whole[...]
            gather_end()
            wide_ref[...] = wide_k[...]

        return carry

    lax.fori_loop(0, STEPS, step, 0)


def factors(weight, sketch):
    vmem = pl.BlockSpec(memory_space=pltpu.VMEM)
    dma = pltpu.SemaphoreType.DMA
    return pl.pallas_call(
        factors_kernel,
        name="factors",
        out_shape=(
            jax.ShapeDtypeStruct((ROWS, RANK), f32),
            jax.ShapeDtypeStruct((PAD, RANK), f32),
            jax.ShapeDtypeStruct((RANK, RANK), f32),
            jax.ShapeDtypeStruct((RANK, RANK), f32),
        ),
        in_specs=[pl.BlockSpec(memory_space=pl.ANY), vmem],
        out_specs=(vmem, vmem, vmem, vmem),
        scratch_shapes=[
            pltpu.VMEM((ROWS, PAD), bf16),
            pltpu.VMEM((PAD, RANK), bf16),
            pltpu.VMEM((ROWS, 2 * RANK), bf16),
            pltpu.VMEM((PAD, RANK), f32),
            pltpu.VMEM((STEPS, 4, TALL, RANK), f32),
            pltpu.VMEM((4, TALL, RANK), f32),
            pltpu.VMEM((STEPS, 4, TALL, RANK), f32),
            pltpu.VMEM((STEPS, ROWS, RANK), f32),
            pltpu.VMEM((PAD, RANK), bf16),
            pltpu.VMEM((PAD, RANK), bf16),
            pltpu.VMEM((STEPS, 4, PART, RANK), bf16),
            pltpu.VMEM((STEPS, 4, PART, RANK), bf16),
            pltpu.VMEM((STEPS, PAD, RANK), f32),
            pltpu.VMEM((OWN, RANK), f32),
            pltpu.VMEM((STEPS * 4, RANK, RANK), f32),
            pltpu.VMEM((STEPS * 4, NCOL, SEG, RANK), f32),
            pltpu.VMEM((STEPS * 4, NROW, SEG, RANK), f32),
            pltpu.VMEM((STEPS * 4, RANK, RANK), f32),
            pltpu.VMEM((RANK, 2 * RANK), f32),
            pltpu.VMEM((RANK, RANK), f32),
            pltpu.VMEM((TALL, RANK), f32),
            pltpu.VMEM((RANK, RANK), f32),
            pltpu.VMEM((RANK, RANK), f32),
            pltpu.VMEM((RANK, RANK), f32),
            pltpu.VMEM((ROWS, RANK), f32),
            dma((4,)),
            dma((STEPS * 4, 3)),
            dma((STEPS * 4, 3)),
            dma((STEPS, 4)),
            dma((STEPS, 4)),
            dma((STEPS,)),
            dma((STEPS,)),
            dma((STEPS, 8)),
            dma((STEPS, 8)),
            dma((STEPS, 6, 4)),
            dma((STEPS, 6, 4)),
            dma((STEPS, 6, 4)),
            dma((STEPS, 6, 4)),
            dma((STEPS, 6, 4)),
            dma((STEPS, 6, 4)),
        ],
        compiler_params=pltpu.CompilerParams(
            collective_id=0, has_side_effects=True, vmem_limit_bytes=60 << 20
        ),
    )(weight, sketch)


def residual_kernel(
    w_hbm, basis_hbm, wide_hbm, half_ref, total_ref, fa_hbm, fb_hbm, res_hbm,
    w_ref, basis_ref, wide_ref, six, left, right, fa_ref, fb_ref, w_sem, in_sem, fa_sem, fb_sem, res_sem,
):
    wide_load = pltpu.make_async_copy(wide_hbm, wide_ref, in_sem.at[0])
    basis_load = pltpu.make_async_copy(basis_hbm, basis_ref, in_sem.at[1])
    wide_load.start()
    basis_load.start()
    loads = []
    for i in range(4):
        at = pl.ds(i * 256, 256)
        loads.append(pltpu.make_async_copy(w_hbm.at[at, :], w_ref.at[at, :], w_sem.at[i]))
        loads[-1].start()
    wide_load.wait()

    def prepare(t):
        at = pl.ds(pl.multiple_of(t * TILE, 128), TILE)
        six[:, at] = right6(wide_ref[at, :].T, 0)

    eye = eye_of()
    half = half_ref[...]
    scale = jnp.sqrt(jnp.sum(half * half, keepdims=True))

    def newton(i, pair):
        prepare(i)
        return newton_step(pair, eye)

    upper, inverse = lax.fori_loop(0, NS_ITERS, newton, (half / scale, eye))
    prepare(NS_ITERS)
    root = jnp.sqrt(scale)
    total = total_ref[...]
    quarter = mm(total.T, upper * root)
    six_left = left6(mm(inverse / root, total), 1)
    basis_load.wait()
    fa_store = pltpu.make_async_copy(fa_ref, fa_hbm, fa_sem)
    for t in range(ROWS // 256):
        at = pl.ds(t * 256, 256)
        a = mm(basis_ref[at, :], quarter)
        fa_ref[at, :] = a
        hi = a.astype(bf16)
        low = (a - hi.astype(f32)).astype(bf16)
        left[at, :] = jnp.concatenate([hi, low, hi], 1)
    fa_store.start()
    stores = [fa_store]
    for load in loads:
        load.wait()
    for t in range(WIDE_TILES):
        at = pl.ds(t * WIDE_TILE, WIDE_TILE)
        b = jnp.dot(six_left, six[:, at], preferred_element_type=f32)
        fb_ref[:, at] = b
        hi = b.astype(bf16)
        low = (b - hi.astype(f32)).astype(bf16)
        right[:, at] = jnp.concatenate([hi, hi, low], 0)
        stores.append(pltpu.make_async_copy(fb_ref.at[:, at], fb_hbm.at[:, at], fb_sem.at[t]))
        stores[-1].start()
        for r in range(2):
            rows = pl.ds(r * (ROWS // 2), ROWS // 2)
            product = jnp.dot(left[rows, :], right[:, at], preferred_element_type=f32)
            w_ref[rows, at] = (w_ref[rows, at].astype(f32) - product).astype(bf16)
            stores.append(pltpu.make_async_copy(w_ref.at[rows, at], res_hbm.at[rows, at], res_sem.at[t, r]))
            stores[-1].start()
    for store in stores:
        store.wait()


def residual(weight, basis, wide, half, total):
    vmem = pl.BlockSpec(memory_space=pltpu.VMEM)
    hbm = pl.BlockSpec(memory_space=pl.ANY)
    dma = pltpu.SemaphoreType.DMA
    return pl.pallas_call(
        residual_kernel,
        name="residual",
        out_shape=(
            jax.ShapeDtypeStruct((ROWS, RANK), f32),
            jax.ShapeDtypeStruct((RANK, COLS), f32),
            jax.ShapeDtypeStruct((ROWS, COLS), bf16),
        ),
        in_specs=[hbm, hbm, hbm, vmem, vmem],
        out_specs=(hbm, hbm, hbm),
        scratch_shapes=[
            pltpu.VMEM((ROWS, COLS), bf16),
            pltpu.VMEM((ROWS, RANK), f32),
            pltpu.VMEM((PAD, RANK), f32),
            pltpu.VMEM((6 * RANK, COLS), bf16),
            pltpu.VMEM((ROWS, 3 * RANK), bf16),
            pltpu.VMEM((3 * RANK, COLS), bf16),
            pltpu.VMEM((ROWS, RANK), f32),
            pltpu.VMEM((RANK, COLS), f32),
            dma((4,)),
            dma((2,)),
            dma,
            dma((WIDE_TILES,)),
            dma((WIDE_TILES, 2)),
        ],
        compiler_params=pltpu.CompilerParams(vmem_limit_bytes=60 << 20),
    )(weight, basis, wide, half, total)


def on_device(weight, sketch):
    return residual(weight, *factors(weight, sketch))


def solution(mesh):
    return jax.shard_map(
        on_device,
        mesh=mesh,
        in_specs=(P("row", "col"), P("col", None)),
        out_specs=(P("row", None), P(None, "col"), P("row", "col")),
        check_vma=False,
    )
```

```python
import jax
import jax.numpy as jnp
from jax import lax
from jax.experimental import pallas as pl
from jax.experimental.pallas import tpu as pltpu
from jax.sharding import PartitionSpec as P

POWER = 2
NS_ITERS = 12
RANK = 128
ROWS = 1024
COLS = 4992
PAD = 5120
NCOL = 8
NROW = 16
PART = PAD // 4
OWN = PAD // NROW
PIECE = PART // NROW
TALL = ROWS // NCOL
SEG = RANK // NCOL
STEPS = POWER + 1
TILE = 512
BLOCK = 32
WIDE_TILES = 3
WIDE_TILE = COLS // WIDE_TILES

f32 = jnp.float32
bf16 = jnp.bfloat16
MESH = pl.DeviceIdType.MESH

ORDER = ((0, 2, 1, 3), (2, 1, 3, 0), (1, 3, 0, 2), (3, 0, 2, 1))

MESSAGES = ((0, 320), (320, 320), (640, 160), (800, 160), (960, 160), (1120, 160))
LOW_FROM = (POWER, POWER, POWER, POWER, 0, 0)
GATHER = (2, 1, 0, 1, 0, 0)


def split3(a):
    hi = a.astype(bf16)
    rest = a - hi.astype(f32)
    mid = rest.astype(bf16)
    low = (rest - mid.astype(f32)).astype(bf16)
    return hi, mid, low


def left6(a, axis):
    hi, mid, low = split3(a)
    return jnp.concatenate([hi, hi, mid, hi, low, mid], axis)


def right6(a, axis):
    hi, mid, low = split3(a)
    return jnp.concatenate([hi, mid, hi, low, hi, mid], axis)


def mm(a, b):
    return jnp.dot(left6(a, 1), right6(b, 0), preferred_element_type=f32)


def gram_of(y):
    return lax.dot_general(
        left6(y, 0), right6(y, 0), (((0,), (0,)), ((), ())), preferred_element_type=f32
    )


def eye_of():
    r = lax.broadcasted_iota(jnp.int32, (RANK, RANK), 0)
    c = lax.broadcasted_iota(jnp.int32, (RANK, RANK), 1)
    return jnp.where(r == c, 1.0, 0.0).astype(f32)


def newton_step(pair, eye):
    upper, inverse = pair
    middle = 1.5 * eye - 0.5 * mm(inverse, upper)
    return mm(upper, middle), mm(middle, inverse)


def cholesky_inverse(gram, s_ref, m_ref):
    s_ref[:, 0:RANK] = gram
    s_ref[:, RANK:] = eye_of()
    sub = lax.broadcasted_iota(jnp.int32, (8, RANK), 0)
    lane = lax.broadcasted_iota(jnp.int32, (BLOCK, RANK), 1)
    groups = range(BLOCK // 8)

    def spread(v, at):
        return jnp.broadcast_to(v[at : at + 1, :], (8, RANK))

    for o in range(0, RANK, BLOCK):
        u = [s_ref[o + 8 * g : o + 8 * g + 8, 0:RANK] for g in groups]
        n = [s_ref[o + 8 * g : o + 8 * g + 8, RANK:] for g in groups]
        square = [
            [jnp.broadcast_to(u[g][:, o + j : o + j + 1], (8, RANK)) if g >= j // 8 else None for g in groups]
            for j in range(BLOCK)
        ]
        scale = [jnp.ones((8, RANK), f32) for _ in groups]
        for j in range(BLOCK):
            top, at = divmod(j, 8)
            pivot = spread(square[j][top], at)
            inverse = 1.0 / pivot
            scale[top] = jnp.where(sub == at, lax.rsqrt(pivot), scale[top])
            u_row, n_row = spread(u[top], at), spread(n[top], at)
            times = {}
            for g in groups[top:]:
                column = square[j][g]
                if g == top:
                    column = jnp.where(sub > at, column, 0.0)
                times[g] = column * inverse
            for c in range(j + 1, BLOCK):
                entry = spread(square[j][c // 8], c % 8)
                for g in groups[c // 8 :]:
                    square[c][g] = square[c][g] - times[g] * entry
            for g in groups[top:]:
                u[g] = u[g] - times[g] * u_row
                n[g] = n[g] - times[g] * n_row
        u = jnp.concatenate([a * b for a, b in zip(u, scale)], 0)
        n = jnp.concatenate([a * b for a, b in zip(n, scale)], 0)
        m_ref[o : o + BLOCK, :] = n
        if o + BLOCK < RANK:
            u = jnp.where(lane >= o + BLOCK, u, 0.0)
            parts = []
            for v in (u, n):
                hi = v.astype(bf16).astype(f32)
                mid = (v - hi).astype(bf16).astype(f32)
                parts.append((hi, mid, v - hi - mid))
            (uh, um, ul), (nh, nm, nl) = parts
            left = jnp.concatenate([uh, uh, um, uh, ul, um], 0)
            right = jnp.concatenate(
                [
                    jnp.concatenate([uh, um, uh, ul, uh, um], 0),
                    jnp.concatenate([nh, nm, nh, nl, nh, nm], 0),
                ],
                1,
            )
            change = lax.dot_general(
                left, right, (((0,), (0,)), ((), ())), preferred_element_type=f32
            )
            s_ref[o + BLOCK :, :] = s_ref[o + BLOCK :, :] - change[o + BLOCK :, :]


def factors_kernel(
    w_hbm, sketch_ref, basis_ref, wide_ref, half_ref, total_ref,
    w_ref, fac, b16, part, core_in, core_sum, tall_in, tall_all, stage_hi, stage_lo, land_hi, land_lo, wide_all,
    own, g_ref, ar1, ar2, ar3, s_ref, m_ref, tall_own, tall_first, tall_second, wide_second, y_ref,
    w_sem, out_sem, ar_send, ar_recv, c_send, c_recv, t_send, t_recv, ta_send, ta_recv, r_send, r_recv, l_send, l_recv, a_send, a_recv,
):
    row = lax.axis_index("row")
    col = lax.axis_index("col")
    y = col // 2
    x = row // 4
    z = row % 4
    partner = ((x + 1 - 2 * (x % 2)) * 4 + z, (3 - x) * 4 + z, x * 4 + z + 1 - 2 * (z % 2), x * 4 + 3 - z)
    xhi, zhi = x // 2, z // 2
    bit = ((x + xhi) % 2, xhi, (z + zhi) % 2, zhi)

    def load(j):
        at = pl.ds(pl.multiple_of((y + 1 + j) % 4 * 2 * TALL, 2 * TALL), 2 * TALL)
        return pltpu.make_async_copy(w_hbm.at[at, :], w_ref.at[at, pl.ds(0, COLS)], w_sem.at[j])

    for j in range(4):
        load(j).start()

    barrier = pltpu.get_barrier_semaphore()
    for d in range(1, NCOL):
        pl.semaphore_signal(barrier, inc=1, device_id={"col": (col + d) % NCOL}, device_id_type=MESH)
    for d in range(1, NROW):
        pl.semaphore_signal(barrier, inc=1, device_id={"row": (row + d) % NROW}, device_id_type=MESH)

    w_ref[:, pl.ds(COLS, PAD - COLS)] = jnp.zeros((ROWS, PAD - COLS), bf16)
    fac[pl.ds(0, COLS), :] = sketch_ref[...]
    fac[pl.ds(COLS, PAD - COLS), :] = jnp.zeros((PAD - COLS, RANK), bf16)
    pl.semaphore_wait(barrier, NCOL + NROW - 2)

    def send(src, dst, send_sem, recv_sem, to):
        pltpu.make_async_remote_copy(
            src_ref=src, dst_ref=dst, send_sem=send_sem, recv_sem=recv_sem, device_id=to, device_id_type=MESH
        ).start()

    def wait(ref, sem):
        pltpu.make_async_copy(ref, ref, sem).wait()

    mine16 = pl.ds(pl.multiple_of(col * SEG, SEG), SEG)

    def sum_start(index):
        for d in range(1, NCOL):
            peer = (col + d) % NCOL
            send(g_ref.at[index, pl.ds(pl.multiple_of(peer * SEG, SEG), SEG), :], ar1.at[index, col],
                 ar_send.at[index, 0], ar_recv.at[index, 0], {"col": peer})
        ar1[index, col] = g_ref[index, mine16, :]

    def sum_row(index):
        wait(ar1.at[index, pl.ds(0, NCOL - 1)], ar_recv.at[index, 0])
        ar2[index, row] = jnp.sum(ar1[index], axis=0)
        for d in range(1, NROW):
            send(ar2.at[index, row], ar2.at[index, row], ar_send.at[index, 1], ar_recv.at[index, 1],
                 {"row": (row + d) % NROW})

    def sum_col(index):
        wait(ar2.at[index, pl.ds(0, NROW - 1)], ar_recv.at[index, 1])
        ar3[index, mine16, :] = jnp.sum(ar2[index], axis=0)
        for d in range(1, NCOL):
            send(ar3.at[index, mine16, :], ar3.at[index, mine16, :], ar_send.at[index, 2], ar_recv.at[index, 2],
                 {"col": (col + d) % NCOL})

    def sum_end(index):
        wait(ar3.at[index, pl.ds(0, SEG * (NCOL - 1)), :], ar_recv.at[index, 2])
        wait(ar1.at[index, pl.ds(0, NCOL - 1)], ar_send.at[index, 0])
        wait(ar2.at[index, pl.ds(0, NROW - 1)], ar_send.at[index, 1])
        wait(ar3.at[index, pl.ds(0, SEG * (NCOL - 1)), :], ar_send.at[index, 2])

    def corrected(index, before):
        return mm(mm(before, ar3[index]), before.T)

    wide_second[...] = eye_of()

    def step(k, carry):
        first_tall, second_tall, first_wide, second_wide = (k * 4 + i for i in range(4))
        last_wide = jnp.maximum(k - 1, 0) * 4 + 3

        mine = pl.ds(pl.multiple_of(col * TALL, TALL), TALL)
        tall_k = tall_in.at[k]

        core = col % 2
        sibling = {"col": col + 1 - 2 * core}

        def chunk(index):
            return pl.ds(pl.multiple_of(index * TALL, TALL), TALL)

        def tall_pair(j, carry):
            pair = (y + 1 + j) % 4
            at = pl.ds(pl.multiple_of(pair * 2 * TALL, 2 * TALL), 2 * TALL)

            @pl.when(k == 0)
            def _():
                load(j).wait()

            y_ref[at, :] = jnp.dot(w_ref[at, :], fac[...], preferred_element_type=f32)
            send(y_ref.at[chunk(pair * 2 + 1 - core), :], core_in.at[k, j], c_send.at[k, j], c_recv.at[k, j], sibling)

            @pl.when(j > 0)
            def _():
                before = (y + j) % 4 * 2 + core
                wait(core_in.at[k, j - 1], c_recv.at[k, j - 1])
                core_sum[j - 1] = y_ref[chunk(before), :] + core_in[k, j - 1]
                send(core_sum.at[j - 1], tall_k.at[y], t_send.at[k], t_recv.at[k], {"col": before})

            return carry

        lax.fori_loop(0, 4, tall_pair, 0)
        wait(core_in.at[k, 3], c_recv.at[k, 3])
        tall_k[y] = y_ref[mine, :] + core_in[k, 3]

        @pl.when(k > 0)
        def _():
            sum_row(last_wide)

        wait(tall_k.at[pl.ds(0, 3)], t_recv.at[k])
        panel = jnp.sum(tall_k[...], axis=0)
        whole = tall_all.at[k]
        whole[mine, :] = panel
        for d in (1, 3, 2):
            send(whole.at[mine, :], whole.at[mine, :], ta_send.at[k, 4 - d], ta_recv.at[k, 4 - d],
                 {"col": (y + d) % 4 * 2 + core})
        send(whole.at[mine, :], whole.at[mine, :], ta_send.at[k, 0], ta_recv.at[k, 0], sibling)
        tall_own[...] = panel
        g_ref[first_tall] = gram_of(panel)
        sum_start(first_tall)

        @pl.when(k > 0)
        def _():
            sum_col(last_wide)

        for d in (1, 3, 2):
            at = chunk((y + d) % 4 * 2 + core)
            wait(whole.at[at, :], ta_recv.at[k, d])
            send(whole.at[at, :], whole.at[at, :], ta_send.at[k, 4 + d], ta_recv.at[k, 4 + d], sibling)
        for d in (0, 5, 6, 7):
            wait(whole.at[mine, :], ta_recv.at[k, d])
        sum_row(first_tall)
        raw = whole[...]
        high = raw.astype(bf16)
        b16[:, 0:RANK] = high
        b16[:, RANK:] = (raw - high.astype(f32)).astype(bf16)

        def times(at):
            both = lax.dot_general(
                w_ref[:, at], b16[...], (((0,), (0,)), ((), ())), preferred_element_type=f32
            )
            part[at, :] = both[:, 0:RANK] + both[:, RANK:]

        def rows_at(offset, size):
            return pl.ds(pl.multiple_of(offset, PIECE), size)

        def post(m, q, kind, offset):
            start, size = MESSAGES[m]
            at = rows_at(offset, size)
            land = pl.ds(start, size)
            value = part[at, :]
            high = value.astype(bf16)
            stage_hi[at, :] = high
            send(stage_hi.at[at, :], land_hi.at[k, q, land, :], r_send.at[k, m, q], r_recv.at[k, m, q],
                 {"row": partner[kind]})

            @pl.when(k >= LOW_FROM[m])
            def _():
                stage_lo[at, :] = (value - high.astype(f32)).astype(bf16)
                send(stage_lo.at[at, :], land_lo.at[k, q, land, :], l_send.at[k, m, q], l_recv.at[k, m, q],
                     {"row": partner[kind]})

        def take(m, q, offset):
            start, size = MESSAGES[m]
            at = rows_at(offset, size)
            land = pl.ds(start, size)
            wait(land_hi.at[k, q, land, :], r_recv.at[k, m, q])
            part[at, :] = part[at, :] + land_hi[k, q, land, :].astype(f32)

            @pl.when(k >= LOW_FROM[m])
            def _():
                wait(land_lo.at[k, q, land, :], l_recv.at[k, m, q])
                part[at, :] = part[at, :] + land_lo[k, q, land, :].astype(f32)

        kinds = ORDER
        half_size, quarter_size, size = PART // 2, PART // 4, PART // 8
        keep0, keep1, send1, keep2, send2 = [], [], [], [], []
        for q in range(4):
            b0, b1, b2 = (bit[kinds[q][s]] for s in range(3))
            away = PART * q + (1 - b0) * half_size
            times(pl.ds(pl.multiple_of(away, 128), half_size))
            post(0, q, kinds[q][0], away + (1 - b1) * quarter_size)
            post(1, q, kinds[q][0], away + b1 * quarter_size)
            keep0.append(PART * q + b0 * half_size)
            send1.append(keep0[q] + (1 - b1) * quarter_size)
            keep1.append(keep0[q] + b1 * quarter_size)
            send2.append(keep1[q] + (1 - b2) * size)
            keep2.append(keep1[q] + b2 * size)
        for q in range(4):
            times(pl.ds(pl.multiple_of(keep0[q], 128), half_size))

        @pl.when(k > 0)
        def _():
            sum_end(last_wide)
            cholesky_inverse(ar3[last_wide], s_ref, wide_second)

        for q in range(4):
            b2 = bit[kinds[q][2]]
            take(0, q, send1[q])
            post(2, q, kinds[q][1], send1[q] + (1 - b2) * size)
            post(3, q, kinds[q][1], send1[q] + b2 * size)
        sum_col(first_tall)
        for q in range(4):
            take(1, q, keep1[q])
        for q in range(4):
            take(2, q, send2[q])
            post(4, q, kinds[q][2], send2[q])
        sum_end(first_tall)
        cholesky_inverse(corrected(first_tall, wide_second[...]), s_ref, m_ref)
        for q in range(4):
            take(3, q, keep2[q])
        for q in range(4):
            take(4, q, keep2[q])
            post(5, q, kinds[q][3], keep2[q])
        tall_first[...] = mm(m_ref[...], wide_second[...])
        g_ref[second_tall] = gram_of(mm(tall_own[...], tall_first[...].T))
        sum_start(second_tall)
        wide_k = wide_all.at[k]
        for q in range(4):
            at = rows_at(keep2[q], size)
            land = pl.ds(*MESSAGES[5])
            wait(land_hi.at[k, q, land, :], r_recv.at[k, 5, q])
            wide_k[at, :] = stage_hi[at, :].astype(f32) + land_hi[k, q, land, :].astype(f32)
            wait(land_lo.at[k, q, land, :], l_recv.at[k, 5, q])
            low = stage_lo[at, :].astype(f32) + land_lo[k, q, land, :].astype(f32)
            wide_k[at, :] = wide_k[at, :] + low

        for q in range(4):
            at = rows_at(keep2[q] + bit[kinds[q][3]] * PIECE, PIECE)
            own[pl.ds(PIECE * q, PIECE), :] = wide_k[at, :]

        def gather(g, offsets, rows):
            for q in range(4):
                at = rows_at(offsets[q], rows)
                send(wide_k.at[at, :], wide_k.at[at, :], a_send.at[k, g, q], a_recv.at[k, g, q],
                     {"row": partner[kinds[q][GATHER[g]]]})

        def gather_wait(g, rows, sem):
            for q in range(4):
                wait(wide_k.at[pl.ds(0, rows), :], sem.at[k, g, q])

        for g in range(3):
            gather(g, keep2, size)
        own[...] = mm(own[...], tall_first[...].T)
        g_ref[first_wide] = gram_of(own[...])
        sum_start(first_wide)
        sum_row(second_tall)
        wait(tall_k.at[pl.ds(0, 3)], t_send.at[k])
        for j in range(4):
            wait(core_in.at[k, j], c_send.at[k, j])
        for d in (0, 1, 2, 3, 5, 6, 7):
            wait(whole.at[mine, :], ta_send.at[k, d])
        for m, (_, rows) in enumerate(MESSAGES):
            for q in range(4):
                wait(stage_hi.at[pl.ds(0, rows), :], r_send.at[k, m, q])

                @pl.when(k >= LOW_FROM[m])
                def _():
                    wait(stage_lo.at[pl.ds(0, rows), :], l_send.at[k, m, q])

        sum_row(first_wide)
        gather_wait(0, size, a_recv)
        gather(3, send2, size)
        gather(4, send2, size)
        sum_col(second_tall)
        sum_col(first_wide)
        gather_wait(1, size, a_recv)
        gather_wait(3, size, a_recv)
        gather(5, send1, 2 * size)
        sum_end(second_tall)
        cholesky_inverse(ar3[second_tall], s_ref, tall_second)

        def gather_end():
            gather_wait(2, size, a_recv)
            gather_wait(4, size, a_recv)
            gather_wait(5, 2 * size, a_recv)
            for g in range(5):
                gather_wait(g, size, a_send)
            gather_wait(5, 2 * size, a_send)

        second = tall_second[...]
        total = mm(second, tall_first[...])
        sum_end(first_wide)
        gram = corrected(first_wide, second)

        @pl.when(k < POWER)
        def _():
            cholesky_inverse(gram, s_ref, m_ref)
            inverse = m_ref[...]
            turned = mm(inverse, total).T
            g_ref[second_wide] = gram_of(mm(own[...], mm(inverse, second).T))
            sum_start(second_wide)
            gather_end()
            right = right6(turned, 0)

            def make_factor(t, carry):
                at = pl.ds(pl.multiple_of(t * 512, 512), 512)
                fac[at, :] = jnp.dot(left6(wide_k[at, :], 1), right, preferred_element_type=f32).astype(bf16)
                return carry

            lax.fori_loop(0, PAD // 512, make_factor, 0)

        @pl.when(k == POWER)
        def _():
            eye = eye_of()
            scale = jnp.sqrt(jnp.sum(gram * gram, keepdims=True))

            def newton(_, pair):
                return newton_step(pair, eye)

            basis_store = pltpu.make_async_copy(whole, basis_ref, out_sem.at[0])
            wide_store = pltpu.make_async_copy(wide_k, wide_ref, out_sem.at[1])
            basis_store.start()
            total_ref[...] = total
            pair = lax.fori_loop(0, NS_ITERS // 2, newton, (gram / scale, eye))
            gather_end()
            wide_store.start()
            pair = lax.fori_loop(0, NS_ITERS - NS_ITERS // 2, newton, pair)
            half_ref[...] = pair[0] * jnp.sqrt(scale)
            basis_store.wait()
            wide_store.wait()

        return carry

    lax.fori_loop(0, STEPS, step, 0)


def factors(weight, sketch):
    vmem = pl.BlockSpec(memory_space=pltpu.VMEM)
    dma = pltpu.SemaphoreType.DMA
    return pl.pallas_call(
        factors_kernel,
        name="factors",
        out_shape=(
            jax.ShapeDtypeStruct((ROWS, RANK), f32),
            jax.ShapeDtypeStruct((PAD, RANK), f32),
            jax.ShapeDtypeStruct((RANK, RANK), f32),
            jax.ShapeDtypeStruct((RANK, RANK), f32),
        ),
        in_specs=[pl.BlockSpec(memory_space=pl.ANY), vmem],
        out_specs=(pl.BlockSpec(memory_space=pl.ANY), pl.BlockSpec(memory_space=pl.ANY), vmem, vmem),
        scratch_shapes=[
            pltpu.VMEM((ROWS, PAD), bf16),
            pltpu.VMEM((PAD, RANK), bf16),
            pltpu.VMEM((ROWS, 2 * RANK), bf16),
            pltpu.VMEM((PAD, RANK), f32),
            pltpu.VMEM((STEPS, 4, TALL, RANK), f32),
            pltpu.VMEM((4, TALL, RANK), f32),
            pltpu.VMEM((STEPS, 4, TALL, RANK), f32),
            pltpu.VMEM((STEPS, ROWS, RANK), f32),
            pltpu.VMEM((PAD, RANK), bf16),
            pltpu.VMEM((PAD, RANK), bf16),
            pltpu.VMEM((STEPS, 4, PART, RANK), bf16),
            pltpu.VMEM((STEPS, 4, PART, RANK), bf16),
            pltpu.VMEM((STEPS, PAD, RANK), f32),
            pltpu.VMEM((OWN, RANK), f32),
            pltpu.VMEM((STEPS * 4, RANK, RANK), f32),
            pltpu.VMEM((STEPS * 4, NCOL, SEG, RANK), f32),
            pltpu.VMEM((STEPS * 4, NROW, SEG, RANK), f32),
            pltpu.VMEM((STEPS * 4, RANK, RANK), f32),
            pltpu.VMEM((RANK, 2 * RANK), f32),
            pltpu.VMEM((RANK, RANK), f32),
            pltpu.VMEM((TALL, RANK), f32),
            pltpu.VMEM((RANK, RANK), f32),
            pltpu.VMEM((RANK, RANK), f32),
            pltpu.VMEM((RANK, RANK), f32),
            pltpu.VMEM((ROWS, RANK), f32),
            dma((4,)),
            dma((2,)),
            dma((STEPS * 4, 3)),
            dma((STEPS * 4, 3)),
            dma((STEPS, 4)),
            dma((STEPS, 4)),
            dma((STEPS,)),
            dma((STEPS,)),
            dma((STEPS, 8)),
            dma((STEPS, 8)),
            dma((STEPS, 6, 4)),
            dma((STEPS, 6, 4)),
            dma((STEPS, 6, 4)),
            dma((STEPS, 6, 4)),
            dma((STEPS, 6, 4)),
            dma((STEPS, 6, 4)),
        ],
        compiler_params=pltpu.CompilerParams(
            collective_id=0, has_side_effects=True, vmem_limit_bytes=60 << 20
        ),
    )(weight, sketch)


def residual_kernel(
    w_hbm, basis_hbm, wide_hbm, half_ref, total_ref, fa_hbm, fb_hbm, res_hbm,
    w_ref, basis_ref, wide_ref, six, left, right, fa_ref, fb_ref, w_sem, in_sem, fa_sem, fb_sem, res_sem,
):
    wide_load = pltpu.make_async_copy(wide_hbm, wide_ref, in_sem.at[0])
    basis_load = pltpu.make_async_copy(basis_hbm, basis_ref, in_sem.at[1])
    wide_load.start()
    basis_load.start()
    loads = []
    for i in range(4):
        at = pl.ds(i * 256, 256)
        loads.append(pltpu.make_async_copy(w_hbm.at[at, :], w_ref.at[at, :], w_sem.at[i]))
        loads[-1].start()

    def prepare(t):
        at = pl.ds(pl.multiple_of(t * TILE, 128), TILE)
        six[:, at] = right6(wide_ref[at, :].T, 0)

    eye = eye_of()
    half = half_ref[...]
    scale = jnp.sqrt(jnp.sum(half * half, keepdims=True))

    def newton(i, pair):
        return newton_step(pair, eye)

    def newton_and_prepare(i, pair):
        prepare(i)
        return newton_step(pair, eye)

    tiles = PAD // TILE
    pair = lax.fori_loop(0, NS_ITERS - tiles, newton, (half / scale, eye))
    wide_load.wait()
    upper, inverse = lax.fori_loop(0, tiles, newton_and_prepare, pair)
    root = jnp.sqrt(scale)
    total = total_ref[...]
    quarter = mm(total.T, upper * root)
    six_left = left6(mm(inverse / root, total), 1)
    basis_load.wait()
    fa_store = pltpu.make_async_copy(fa_ref, fa_hbm, fa_sem)
    for t in range(ROWS // 256):
        at = pl.ds(t * 256, 256)
        a = mm(basis_ref[at, :], quarter)
        fa_ref[at, :] = a
        hi = a.astype(bf16)
        low = (a - hi.astype(f32)).astype(bf16)
        left[at, :] = jnp.concatenate([hi, low, hi], 1)
    fa_store.start()
    stores = [fa_store]
    for load in loads:
        load.wait()
    for t in range(WIDE_TILES):
        at = pl.ds(t * WIDE_TILE, WIDE_TILE)
        b = jnp.dot(six_left, six[:, at], preferred_element_type=f32)
        fb_ref[:, at] = b
        hi = b.astype(bf16)
        low = (b - hi.astype(f32)).astype(bf16)
        right[:, at] = jnp.concatenate([hi, hi, low], 0)
        stores.append(pltpu.make_async_copy(fb_ref.at[:, at], fb_hbm.at[:, at], fb_sem.at[t]))
        stores[-1].start()
        for r in range(2):
            rows = pl.ds(r * (ROWS // 2), ROWS // 2)
            product = jnp.dot(left[rows, :], right[:, at], preferred_element_type=f32)
            w_ref[rows, at] = (w_ref[rows, at].astype(f32) - product).astype(bf16)
            stores.append(pltpu.make_async_copy(w_ref.at[rows, at], res_hbm.at[rows, at], res_sem.at[t, r]))
            stores[-1].start()
    for store in stores:
        store.wait()


def residual(weight, basis, wide, half, total):
    vmem = pl.BlockSpec(memory_space=pltpu.VMEM)
    hbm = pl.BlockSpec(memory_space=pl.ANY)
    dma = pltpu.SemaphoreType.DMA
    return pl.pallas_call(
        residual_kernel,
        name="residual",
        out_shape=(
            jax.ShapeDtypeStruct((ROWS, RANK), f32),
            jax.ShapeDtypeStruct((RANK, COLS), f32),
            jax.ShapeDtypeStruct((ROWS, COLS), bf16),
        ),
        in_specs=[hbm, hbm, hbm, vmem, vmem],
        out_specs=(hbm, hbm, hbm),
        scratch_shapes=[
            pltpu.VMEM((ROWS, COLS), bf16),
            pltpu.VMEM((ROWS, RANK), f32),
            pltpu.VMEM((PAD, RANK), f32),
            pltpu.VMEM((6 * RANK, PAD), bf16),
            pltpu.VMEM((ROWS, 3 * RANK), bf16),
            pltpu.VMEM((3 * RANK, COLS), bf16),
            pltpu.VMEM((ROWS, RANK), f32),
            pltpu.VMEM((RANK, COLS), f32),
            dma((4,)),
            dma((2,)),
            dma,
            dma((WIDE_TILES,)),
            dma((WIDE_TILES, 2)),
        ],
        compiler_params=pltpu.CompilerParams(vmem_limit_bytes=60 << 20),
    )(weight, basis, wide, half, total)


def on_device(weight, sketch):
    return residual(weight, *factors(weight, sketch))


def solution(mesh):
    return jax.shard_map(
        on_device,
        mesh=mesh,
        in_specs=(P("row", "col"), P("col", None)),
        out_specs=(P("row", None), P(None, "col"), P("row", "col")),
        check_vma=False,
    )
```
